128 devices in a mesh: nest: 2 (over y_hi), gx: 64 (over y_lo, x, z, core).
Axes of the slice: x: 4, y: 4 (y_hi: 2, y_lo: 2; y = y_hi * 2 + y_lo), z: 4, core: 2. Of those that a mesh axis runs over, the one named last changes fastest.
Arguments:
- velocity: float32 [2, 3, 8, 1024, 2048], P('nest', None, None, 'gx'), may hold values from -6 to 6
- viscosity: float32 [2, 8, 1024, 2048], P('nest', None, 'gx'), may hold values from 0.02 to 0.5
- heights: int32 [2, 1024, 2048], P('nest', 'gx'), may hold values from 0 to 4
- row_offset: int32 [1], replicated, may hold values from 0 to 512
- column_offset: int32 [1], replicated, may hold values from 0 to 2047
Outputs:
- new_velocity: float32 [2, 3, 8, 1024, 2048], P('nest', None, None, 'gx')
- pressure: float32 [2, 8, 1024, 2048], P('nest', None, 'gx')
The draws below stay inside these ranges and needn't reach their ends.
All inputs are finite; a program needn't handle non-finite values.
Results may differ from the reference program's by a relative error of at most 0.00012.
Values sent between devices are 32-bit elements; how exact they have to be, the bound alone decides.
A program may use at most 192 MiB of HBM per device.

```python
import math
import jax
import jax.numpy as jnp
from jax import lax

NY = 2048
NZ = 8
NX = 1024
HALF_Y = 1024


def with_ends(values, key, low, high):
    place = [jax.random.randint(jax.random.fold_in(key, axis), (), 0, length) for axis, length in enumerate(values.shape)]
    main_axis = values.shape.index(max(values.shape))
    beside = place[:main_axis] + [(place[main_axis] + 1) % values.shape[main_axis]] + place[main_axis + 1:]
    return values.at[tuple(place)].set(low).at[tuple(beside)].set(high)


def block_levels(rng, shape, cuts, least, largest):
    def one(position, parts):
        draws = jax.random.uniform(jax.random.fold_in(jax.random.fold_in(rng, 6), position), (parts,), jnp.float32, least / len(cuts), largest / len(cuts))
        return jnp.repeat(jnp.exp(draws), shape[position] // parts).reshape((-1,) + (1,) * (len(shape) - position - 1))

    gain = one(*cuts[0])
    for cut in cuts[1:]:
        gain = gain * one(*cut)
    return gain


def normal_values(own_key, dims, scale, bound, pieces=(), held_as=jnp.bfloat16):
    loudness = block_levels(own_key, dims, pieces, -0.22, 0.18) if pieces else 1.0
    array = jax.random.normal(own_key, dims, jnp.float32) * scale * loudness
    return jnp.minimum(jnp.maximum(array, -bound), bound).astype(held_as)


def setup_inputs(seed: int = 0) -> dict:
    seeds = jax.random.split(jax.random.key(seed), 6)
    return {
        "velocity": normal_values(seeds[0], (2, 3, NZ, NX, NY), 1.0, 6.0, ((0, 2), (3, 64)), jnp.float32),
        "viscosity": jnp.clip(jnp.exp(math.log(0.5) - 3.218876 * jax.random.uniform(seeds[1], (2, NZ, NX, NY), jnp.float32) ** block_levels(seeds[1], (2, NZ, NX, NY), ((0, 2), (2, 64)), -0.2, 0.2)), 0.02, 0.5),
        "heights": with_ends(jax.random.randint(seeds[2], (2, NX, NY), 0, NZ // 2 + 1), jax.random.fold_in(seeds[2], 1), 0, (NZ // 2 + 1) - 1).astype(jnp.int32),
        "row_offset": jax.random.randint(seeds[3], (1,), 0, NX // 2 + 1).astype(jnp.int32),
        "column_offset": jax.random.randint(seeds[4], (1,), 0, NY).astype(jnp.int32),
    }


time_step = 0.2
blend_rate = 0.5


def open_cells(roof_level, levels):
    level_index = jnp.arange(levels, dtype=jnp.int32)[:, None, None]
    return (level_index >= roof_level[None]).astype(jnp.float32)


def wrap_rows(field):
    return jnp.concatenate([field[..., -1:, :], field, field[..., :1, :]], axis=-2)


def advance(flow_ext, kappa_ext):
    flow = flow_ext[:, :, 1:-1]
    kappa = kappa_ext[:, 1:-1]
    east_cells = flow_ext[:, :, 2:]
    west_cells = flow_ext[:, :, :-2]
    north_cells = jnp.roll(flow, -1, axis=3)
    south_cells = jnp.roll(flow, 1, axis=3)
    blank = jnp.zeros_like(flow[:, :1])
    upper_cells = jnp.concatenate([flow[:, 1:], blank], axis=1)
    lower_cells = jnp.concatenate([blank, flow[:, :-1]], axis=1)
    face_east = 0.5 * (kappa + kappa_ext[:, 2:])
    face_west = 0.5 * (kappa + kappa_ext[:, :-2])
    face_north = 0.5 * (kappa + jnp.roll(kappa, -1, axis=2))
    face_south = 0.5 * (kappa + jnp.roll(kappa, 1, axis=2))
    face_top = 0.5 * (kappa + jnp.concatenate([kappa[1:], kappa[-1:]], axis=0))
    face_bottom = 0.5 * (kappa + jnp.concatenate([kappa[:1], kappa[:-1]], axis=0))
    carried = 0.5 * (flow[0] * (east_cells - west_cells) + flow[1] * (north_cells - south_cells)
                     + flow[2] * (upper_cells - lower_cells))
    spread = face_east * (east_cells - flow) - face_west * (flow - west_cells)
    spread = spread + face_north * (north_cells - flow) - face_south * (flow - south_cells)
    spread = spread + face_top * (upper_cells - flow) - face_bottom * (flow - lower_cells)
    return flow + time_step * (spread - carried)


def take_footprint(provisional, column_start, half_y):
    columns = provisional.shape[3]
    indices = (column_start + jnp.arange(half_y, dtype=jnp.int32)) % columns
    return jnp.take(provisional, indices, axis=3)


def average_pairs(provisional):
    return 0.5 * (provisional[..., 0::2] + provisional[..., 1::2])


def alternate_rows(rows):
    following = jnp.concatenate([rows[:, :, 1:], rows[:, :, -1:]], axis=2)
    odd_values = 0.5 * (rows + following)
    shape = rows.shape
    return jnp.stack([rows, odd_values], axis=3).reshape(shape[0], shape[1], 2 * shape[2], shape[3])


def relax_child(provisional, incoming, row_start, x_total):
    columns = provisional.shape[3]
    row_count = provisional.shape[2]
    following = jnp.concatenate([incoming[..., 1:], incoming[..., -1:]], axis=-1)
    odd_values = 0.5 * (incoming + following)
    interpolated = jnp.stack([incoming, odd_values], axis=-1).reshape(provisional.shape)
    y_index = jnp.arange(columns, dtype=jnp.int32)
    x_index = row_start + jnp.arange(row_count, dtype=jnp.int32)
    distance_y = jnp.minimum(y_index, columns - 1 - y_index)
    distance_x = jnp.minimum(x_index, x_total - 1 - x_index)
    distance = jnp.minimum(distance_x[:, None], distance_y[None, :]).astype(jnp.float32)
    relax_rate = 0.2 + 0.8 * jnp.exp(-distance * (16.0 / columns))
    return provisional + relax_rate * (interpolated - provisional)


def relax_parent(provisional, incoming, column_start, inside_rows):
    columns = provisional.shape[3]
    half_y = incoming.shape[3]
    y_index = jnp.arange(columns, dtype=jnp.int32)
    local_j = (y_index - column_start) % columns
    inside = inside_rows[:, None] & (local_j < half_y)[None, :]
    clamped = jnp.minimum(local_j, half_y - 1)
    values = jnp.take(incoming, clamped, axis=3)
    return provisional + blend_rate * jnp.where(inside[None, None], values - provisional, 0.0)


def thomas(levels, eigen):
    count = len(levels)
    pivots = []
    partials = []
    for level in range(count):
        diagonal = -1.0 - eigen if level == 0 else -2.0 - eigen
        if level == 0:
            pivot = diagonal
            scaled = levels[0] / pivot
        else:
            pivot = diagonal - 1.0 / pivots[-1]
            scaled = (levels[level] - partials[-1]) / pivot
        pivots.append(pivot)
        partials.append(scaled)
    result = [None] * count
    result[count - 1] = partials[count - 1]
    for level in range(count - 2, -1, -1):
        result[level] = partials[level] - result[level + 1] / pivots[level]
    return result


def hartley(field, axis):
    spectrum = jnp.fft.fft(field, axis=axis)
    return jnp.real(spectrum) - jnp.imag(spectrum)


def project(coupled, fluid_mask):
    flow_x, flow_y, flow_z = coupled[0], coupled[1], coupled[2]
    diff_x = flow_x - jnp.roll(flow_x, 1, axis=1)
    diff_y = flow_y - jnp.roll(flow_y, 1, axis=2)
    diff_z = flow_z - jnp.concatenate([jnp.zeros_like(flow_z[:1]), flow_z[:-1]], axis=0)
    source = ((diff_x + diff_y) + diff_z) / time_step
    spectral = hartley(hartley(source, 2), 1)
    wave_x = jnp.arange(NX, dtype=jnp.int32).astype(jnp.float32)
    wave_y = jnp.arange(NY, dtype=jnp.int32).astype(jnp.float32)
    eigen = 4.0 * jnp.square(jnp.sin(wave_x * (math.pi / NX)))[:, None] + 4.0 * jnp.square(jnp.sin(wave_y * (math.pi / NY)))[None, :]
    solved = jnp.stack(thomas([spectral[level] for level in range(NZ)], eigen), axis=0)
    pressure = hartley(hartley(solved, 1), 2) / (NX * NY)
    grad_x = jnp.roll(pressure, -1, axis=1) - pressure
    grad_y = jnp.roll(pressure, -1, axis=2) - pressure
    grad_z = jnp.concatenate([pressure[1:], jnp.zeros_like(pressure[:1])], axis=0) - pressure
    updated = fluid_mask * (coupled - time_step * jnp.stack([grad_x, grad_y, grad_z], axis=0))
    return updated, pressure


def reference(velocity, viscosity, heights, row_offset, column_offset):
    provisional = []
    masks = []
    for domain in range(2):
        fluid_mask = open_cells(heights[domain], NZ)
        provisional.append(advance(wrap_rows(velocity[domain]), wrap_rows(viscosity[domain])) * fluid_mask)
        masks.append(fluid_mask)
    row_start = row_offset[0]
    column_start = column_offset[0]
    footprint = take_footprint(provisional[0], column_start, HALF_Y)
    under_child = lax.dynamic_slice_in_dim(footprint, row_start, NX // 2, axis=2)
    widened = alternate_rows(under_child)
    halved = average_pairs(provisional[1])
    averaged = 0.5 * (halved[:, :, 0::2] + halved[:, :, 1::2])
    placed = lax.dynamic_update_slice_in_dim(jnp.zeros_like(halved), averaged, row_start, axis=2)
    x_index = jnp.arange(NX, dtype=jnp.int32)
    inside_rows = (x_index >= row_start) & (x_index < row_start + NX // 2)
    coupled = [relax_parent(provisional[0], placed, column_start, inside_rows) * masks[0],
               relax_child(provisional[1], widened, jnp.int32(0), NX) * masks[1]]
    results = []
    pressures = []
    for domain in range(2):
        updated, pressure = project(coupled[domain], masks[domain])
        results.append(updated)
        pressures.append(pressure)
    return jnp.stack(results, axis=0), jnp.stack(pressures, axis=0)
```

```python
import functools
import math

import jax
import jax.numpy as jnp
import ml_dtypes
import numpy as np
from jax import lax
from jax.experimental import pallas as pl
from jax.experimental.pallas import tpu as pltpu
from jax.sharding import PartitionSpec as P

LEVELS = 8
ROWS = 16
LANES = 128
EXTRA = 144
DT = 0.2
BLEND = 0.5
f32 = jnp.float32
bf16 = jnp.bfloat16
VMEM_SPEC = pl.BlockSpec(memory_space=pltpu.VMEM)
SMEM_SPEC = pl.BlockSpec(memory_space=pltpu.SMEM)
ANY_SPEC = pl.BlockSpec(memory_space=pl.ANY)
PARAMS = dict(vmem_limit_bytes=50 * 1024 * 1024)


def split_np(table):
    high = table.astype(ml_dtypes.bfloat16)
    low = (table - high.astype(np.float64)).astype(ml_dtypes.bfloat16)
    return high, low


def split(value):
    high = value.astype(bf16)
    low = (value - high.astype(f32)).astype(bf16)
    return high, low


def cas(angle):
    return np.cos(angle) + np.sin(angle)


@functools.lru_cache(maxsize=None)
def tables(x_total, columns, group):
    half = columns // 2
    m = np.arange(half)
    even = cas(2 * np.pi * ((m[:, None] * m[None, :]) % half) / half)
    odd_index = ((2 * m[:, None] + 1) * (2 * m[None, :] + 1)) % (2 * columns)
    odd = cas(2 * np.pi * odd_index / (2 * columns))
    even_high, even_low = split_np(even)
    odd_high, odd_low = split_np(odd)
    y_tables = np.stack([even_high, even_low, odd_high, odd_low])
    j = np.arange(LEVELS)
    z_vectors = math.sqrt(4 / 17) * np.cos((2 * j[:, None] + 1) * (2 * j[None, :] + 1) * np.pi / 34)
    z_values = 2 - 2 * np.cos((2 * j + 1) * np.pi / 17)
    turn = np.zeros((EXTRA, EXTRA))
    for x in range(ROWS + 1):
        for level in range(LEVELS):
            place = level * ROWS + x if x < ROWS else ROWS * LEVELS + level
            turn[x * LEVELS : x * LEVELS + LEVELS, place] = z_vectors[:, level]
    turn_high, turn_low = split_np(turn)
    back_high, back_low = split_np(turn.T)
    turn_stack = np.concatenate([turn_high, turn_low])
    back_stack = np.concatenate([back_high, back_low])
    wave = np.concatenate([2 * m, 2 * m + 1])
    mu = 4 * np.sin(np.pi * wave / columns)[None, :] ** 2 + z_values[:, None]
    root = 1 + mu / 2 - np.sqrt(mu + mu * mu / 4)
    scale = -1 / (1 / root - root) / columns
    modes = np.stack([root, scale]).astype(np.float32)
    reach = root**ROWS
    tiles = columns // LANES
    jump = np.stack([reach, 1 / (1 - reach**group)])
    jump = jump.reshape(2, LEVELS, tiles, LANES).transpose(2, 0, 1, 3).astype(np.float32)
    wide = np.zeros((2, 256, 256))
    for y in range(256):
        if y % 2 == 0:
            wide[:, y // 2, y] = 1
        else:
            wide[:, y // 2, y] = 0.5
            wide[0, y // 2 + 1, y] = 0.5
            wide[1, min(y // 2 + 1, 127), y] += 0.5
    pair = np.zeros((256, LANES))
    pair[np.arange(256), np.arange(256) // 2] = 0.5
    return dict(
        y=y_tables,
        turn=turn_stack,
        back=back_stack,
        modes=modes,
        jump=jump,
        wide=wide.astype(ml_dtypes.bfloat16),
        pair=pair.astype(ml_dtypes.bfloat16),
    )


def mxu(left, right):
    return jnp.dot(left, right, preferred_element_type=f32)


def halo_kernel(vel, visc, west, east, edge, sems):
    me = lax.axis_index("gx")
    group = lax.axis_size("gx")
    for c in range(3):
        edge[0, c] = vel[c, :, 0, :]
        edge[1, c] = vel[c, :, ROWS - 1, :]
    edge[0, 3] = visc[:, 0, :]
    edge[1, 3] = visc[:, ROWS - 1, :]
    right = lax.rem(me + 1, group)
    left = lax.rem(me + group - 1, group)
    to_right = pltpu.make_async_remote_copy(
        edge.at[1], west, sems.at[0], sems.at[1], device_id={"gx": right},
        device_id_type=pl.DeviceIdType.MESH,
    )
    to_left = pltpu.make_async_remote_copy(
        edge.at[0], east, sems.at[2], sems.at[3], device_id={"gx": left},
        device_id_type=pl.DeviceIdType.MESH,
    )
    to_right.start()
    to_left.start()
    to_right.wait()
    to_left.wait()


def stencil_kernel(oy_ref, vel, visc, heights, west, east, pair, prov, out, mean, tile):
    columns = vel.shape[-1]
    tiles = columns // LANES
    blocks = columns // 256
    is_child = lax.axis_index("nest") == 1
    row = lax.broadcasted_iota(jnp.int32, (ROWS, 256), 0)
    lane = lax.broadcasted_iota(jnp.int32, (ROWS, LANES), 1)

    def cell(i, carry):
        z = i // blocks
        start = pl.multiple_of(lax.rem(i, blocks) * 256, 256)
        here = pl.ds(start, 256)
        before = pl.ds(pl.multiple_of(lax.rem(start + columns - LANES, columns), LANES), LANES)
        after = pl.ds(pl.multiple_of(lax.rem(start + 256, columns), LANES), LANES)
        up = jnp.minimum(z + 1, LEVELS - 1)
        down = jnp.maximum(z - 1, 0)
        up_open = jnp.where(z < LEVELS - 1, 1.0, 0.0).astype(f32)
        down_open = jnp.where(z > 0, 1.0, 0.0).astype(f32)

        def around(ref, lead, c):
            mid = ref[lead + (z, slice(None), here)]
            wide = jnp.concatenate(
                [ref[lead + (z, slice(None), before)], mid, ref[lead + (z, slice(None), after)]],
                axis=1,
            )
            north = pltpu.roll(wide, 511, 1)[:, LANES : LANES + 256]
            south = pltpu.roll(wide, 1, 1)[:, LANES : LANES + 256]
            plus = jnp.where(row == ROWS - 1, east[c, pl.ds(z, 1), here], pltpu.roll(mid, ROWS - 1, 0))
            minus = jnp.where(row == 0, west[c, pl.ds(z, 1), here], pltpu.roll(mid, 1, 0))
            top = ref[lead + (up, slice(None), here)]
            bottom = ref[lead + (down, slice(None), here)]
            return mid, plus, minus, north, south, top, bottom

        k, ke, kw, kn, ks, kt, kb = around(visc, (), 3)
        flow = [around(vel, (c,), c) for c in range(3)]
        half = 0.5 * DT
        kh = half * k
        b0, b1, b2 = (half * flow[c][0] for c in range(3))
        ae = (kh + half * ke) - b0
        aw = (kh + half * kw) + b0
        an = (kh + half * kn) - b1
        as_ = (kh + half * ks) + b1
        at = (kh + half * kt) - b2
        ab = (kh + half * kb) + b2
        mask = jnp.where(z >= heights[:, here], 1.0, 0.0).astype(f32)
        own = 1.0 - (((ae + aw) + (an + as_)) + (at + ab))
        at = at * up_open
        ab = ab * down_open
        for c in range(3):
            mid, plus, minus, north, south, top, bottom = flow[c]
            value = own * mid + ae * plus + aw * minus + an * north + as_ * south + at * top + ab * bottom
            prov[c, z, :, here] = value * mask
        return carry

    lax.fori_loop(0, LEVELS * blocks, cell, 0)

    @pl.when(jnp.logical_not(is_child))
    def _():
        oy = oy_ref[0]
        first = oy // LANES
        shift = lax.rem(oy, LANES)
        turn = lax.rem(LANES - shift, LANES)

        def unit(i, carry):
            cz = i // blocks
            b = lax.rem(i, blocks)
            c = cz // LEVELS
            z = lax.rem(cz, LEVELS)
            one = pl.ds(pl.multiple_of(lax.rem(first + b, tiles) * LANES, LANES), LANES)
            two = pl.ds(pl.multiple_of(lax.rem(first + b + 1, tiles) * LANES, LANES), LANES)
            low = pltpu.roll(prov[c, z, :, one], turn, 1)
            high = pltpu.roll(prov[c, z, :, two], turn, 1)
            out[b * 8 + cz // 3, lax.rem(cz, 3)] = jnp.where(lane < LANES - shift, low, high)
            return carry

        lax.fori_loop(0, 24 * blocks, unit, 0)

    @pl.when(is_child)
    def _():
        def rows(cz, carry):
            c = cz // LEVELS
            z = lax.rem(cz, LEVELS)
            for t in range(tiles):
                cols = pl.ds(t * LANES, LANES)
                tile[t] = prov[c, z, :, cols]
                evens = tile[t, pl.ds(0, 8, stride=2), :]
                odds = tile[t, pl.ds(1, 8, stride=2), :]
                mean[pl.ds(pl.multiple_of(cz * 8, 8), 8), cols] = 0.5 * (evens + odds)
            return carry

        lax.fori_loop(0, 24, rows, 0)
        for b in range(blocks):
            high, low = split(mean[:, pl.ds(b * 256, 256)])
            value = mxu(high, pair[...]) + mxu(low, pair[...])
            out[pl.ds(b * 8, 8), :, pl.ds(0, 8), :] = value.reshape(8, 3, 8, LANES)


def remote(src, dst, send, recv, nest, k):
    return pltpu.make_async_remote_copy(
        src, dst, send, recv, device_id={"nest": nest, "gx": k},
        device_id_type=pl.DeviceIdType.MESH,
    )


def await_bytes(ref, sem):
    pltpu.make_async_copy(ref, ref, sem).wait()


def gather_kernel(src, under, above, sems):
    group = src.shape[0]
    x_total = group * ROWS
    half = x_total // 2
    me = lax.axis_index("gx")
    nest = lax.axis_index("nest")
    here = pl.ds(pl.multiple_of(me * ROWS, ROWS), ROWS)

    @pl.when(nest == 0)
    def _():
        def send_rows(i, carry):
            k = lax.rem(me + i, group)
            remote(src.at[k], under.at[:, here], sems.at[0], sems.at[1], 0, k).start()
            return carry

        lax.fori_loop(1, group, send_rows, 0)
        pltpu.make_async_copy(src.at[me], under.at[:, here], sems.at[1]).start()
        blank = jnp.zeros((3, ROWS, LANES), f32)
        under[:, pl.ds(x_total, ROWS)] = blank
        above[:, pl.ds(0, ROWS)] = blank
        above[:, pl.ds(ROWS + half, ROWS)] = blank
        above[:, pl.ds(2 * ROWS + half, ROWS)] = blank
        await_bytes(src.at[pl.ds(0, group - 1)], sems.at[0])
        await_bytes(under.at[:, pl.ds(0, x_total)], sems.at[1])
        await_bytes(above.at[:, pl.ds(ROWS, half)], sems.at[2])

    @pl.when(nest == 1)
    def _():
        slot = pl.ds(pl.multiple_of(ROWS + me * 8, 8), 8)

        def send_means(i, carry):
            k = lax.rem(me + i, group)
            remote(src.at[k, :, pl.ds(0, 8)], above.at[:, slot], sems.at[0], sems.at[2], 0, k).start()
            return carry

        lax.fori_loop(0, group, send_means, 0)
        await_bytes(src.at[:, :, pl.ds(0, 8)], sems.at[0])


def shift_kernel(ox_ref, under, above, to_child, to_parent):
    group = to_child.shape[0]
    half = group * ROWS // 2

    @pl.when(lax.axis_index("nest") == 0)
    def _():
        ox = ox_ref[0]

        def fill(g, carry):
            rows = pl.ds(pl.multiple_of((ox // 8 + g) * 8, 8), 16)
            first = jnp.clip(ROWS * g - ox + ROWS, 0, half + ROWS)
            back = pl.ds(pl.multiple_of(first // 8 * 8, 8), 24)
            for u in range(3):
                moved = pltpu.roll(under[u, rows], lax.rem(16 - lax.rem(ox, 8), 16), 0)
                to_child[g, pl.ds(u * 9, 9)] = moved[:9]
                moved = pltpu.roll(above[u, back], lax.rem(24 - lax.rem(first, 8), 24), 0)
                to_parent[g, pl.ds(u * ROWS, ROWS)] = moved[:ROWS]
            return carry

        lax.fori_loop(0, group, fill, 0)


def scatter_kernel(to_child, to_parent, dst, sems):
    group = to_child.shape[0]
    me = lax.axis_index("gx")
    nest = lax.axis_index("nest")

    @pl.when(nest == 0)
    def _():
        def send(i, carry):
            k = lax.rem(me + i, group)
            remote(to_child.at[k], dst.at[me, pl.ds(0, 32)], sems.at[0], sems.at[1], 1, k).start()

            @pl.when(i > 0)
            def _():
                remote(to_parent.at[k], dst.at[me], sems.at[2], sems.at[1], 0, k).start()

            return carry

        lax.fori_loop(0, group, send, 0)
        pltpu.make_async_copy(to_parent.at[me], dst.at[me], sems.at[1]).start()
        await_bytes(to_child, sems.at[0])
        await_bytes(to_parent.at[pl.ds(0, group - 1)], sems.at[2])
        await_bytes(dst, sems.at[1])

    @pl.when(nest == 1)
    def _():
        await_bytes(dst.at[:, pl.ds(0, 32)], sems.at[1])


def forward_kernel(
    ox_ref, oy_ref, prov, got, heights, wide_t, turn_t, modes, y_any,
    coupled, spectrum, ends, y_t, mapped, wide, rate, source, turned, sem,
):
    columns = prov.shape[-1]
    group = got.shape[0]
    x_total = group * ROWS
    half = columns // 2
    tiles = columns // LANES
    blocks = columns // 256
    load = pltpu.make_async_copy(y_any, y_t, sem)
    load.start()
    me = lax.axis_index("gx")
    is_child = lax.axis_index("nest") == 1
    ox = ox_ref[0]
    oy = oy_ref[0]
    lane = lax.broadcasted_iota(jnp.int32, (ROWS, LANES), 1)
    row = lax.broadcasted_iota(jnp.int32, (ROWS, LANES), 0)

    @pl.when(is_child)
    def _():
        for b in range(blocks):
            left = got[pl.ds(b * 8, 8), pl.ds(0, 32), :].reshape(256, LANES)
            nxt = min(b + 1, blocks - 1)
            right = got[pl.ds(nxt * 8, 8), pl.ds(0, 32), :].reshape(256, LANES)
            high, low = split(jnp.concatenate([left, right], axis=1))
            table = wide_t[0 if b < blocks - 1 else 1]
            wide[:, :, pl.ds(b * 256, 256)] = (mxu(high, table) + mxu(low, table)).reshape(8, 32, 256)
        last = me == group - 1

        def unit(kz, carry):
            for u in range(3):
                cz = kz * 3 + u
                for t in range(tiles):
                    cols = pl.ds(t * LANES, LANES)
                    own = wide[kz, pl.ds(u * 9, 8), cols]
                    after = wide[kz, pl.ds(u * 9 + 1, 8), cols]
                    tail = lax.broadcasted_iota(jnp.int32, (8, LANES), 0) == 7
                    after = jnp.where(jnp.logical_and(tail, last), own, after)
                    mapped[cz, t, pl.ds(0, 8, stride=2), :] = own
                    mapped[cz, t, pl.ds(1, 8, stride=2), :] = 0.5 * (own + after)
            return carry

        lax.fori_loop(0, 8, unit, 0)

        def rates(t, carry):
            cols = pl.ds(pl.multiple_of(t * LANES, LANES), LANES)
            x = me * ROWS + row
            y = t * LANES + lane
            near_y = jnp.minimum(y, columns - 1 - y)
            near_x = jnp.minimum(x, x_total - 1 - x)
            near = jnp.minimum(near_x, near_y).astype(f32)
            rate[:, cols] = 0.2 + 0.8 * jnp.exp(-near * (16.0 / columns))
            return carry

        lax.fori_loop(0, tiles, rates, 0)

    @pl.when(jnp.logical_not(is_child))
    def _():
        first = oy // LANES
        shift = lax.rem(oy, LANES)

        def unit(i, carry):
            cz = i // tiles
            t = lax.rem(i, tiles)
            at = lax.rem(t - first + tiles, tiles)
            low = jnp.minimum(at, blocks - 1)
            high = jnp.minimum(lax.rem(at + tiles - 1, tiles), blocks - 1)
            kz = cz // 3
            rows = pl.ds(pl.multiple_of(lax.rem(cz, 3) * ROWS, ROWS), ROWS)
            one = pltpu.roll(got[low * 8 + kz, rows, :], shift, 1)
            two = pltpu.roll(got[high * 8 + kz, rows, :], shift, 1)
            mapped[cz, t] = jnp.where(lane >= shift, one, two)
            return carry

        lax.fori_loop(0, 24 * tiles, unit, 0)

        def rates(t, carry):
            cols = pl.ds(pl.multiple_of(t * LANES, LANES), LANES)
            x = me * ROWS + row
            y = t * LANES + lane
            j = y - oy
            j = jnp.where(j < 0, j + columns, j)
            inside = (x >= ox) & (x < ox + x_total // 2) & (j < half)
            rate[:, cols] = jnp.where(inside, BLEND, 0.0)
            return carry

        lax.fori_loop(0, tiles, rates, 0)

    source[pl.ds(ROWS * LEVELS, ROWS), :] = jnp.zeros((ROWS, columns), f32)

    def blend(i, carry):
        z = i // blocks
        b = lax.rem(i, blocks)
        cols = pl.ds(pl.multiple_of(b * 256, 256), 256)
        weight = rate[:, cols]
        mask = jnp.where(z >= heights[:, cols], 1.0, 0.0).astype(f32)
        for c in range(3):
            own = prov[c, z, :, cols]
            other = jnp.concatenate([mapped[c * LEVELS + z, 2 * b], mapped[c * LEVELS + z, 2 * b + 1]], axis=1)
            change = jnp.where(weight > 0.0, other - own, 0.0)
            coupled[c, z, :, cols] = (own + weight * change) * mask
        return carry

    lax.fori_loop(0, LEVELS * blocks, blend, 0)
    row2 = lax.broadcasted_iota(jnp.int32, (ROWS, 256), 0)

    def diverge(i, carry):
        z = i // blocks
        start = pl.multiple_of(lax.rem(i, blocks) * 256, 256)
        cols = pl.ds(start, 256)
        before = pl.ds(pl.multiple_of(lax.rem(start + columns - LANES, columns), LANES), LANES)
        flow_x = coupled[0, z, :, cols]
        flow_y = coupled[1, z, :, cols]
        flow_z = coupled[2, z, :, cols]
        beyond = jnp.concatenate([coupled[1, z, :, before], flow_y], axis=1)
        south = pltpu.roll(beyond, 1, 1)[:, LANES:]
        west = jnp.where(row2 == 0, 0.0, pltpu.roll(flow_x, 1, 0))
        under = coupled[2, jnp.maximum(z - 1, 0), :, cols] * jnp.where(z > 0, 1.0, 0.0).astype(f32)
        value = ((flow_x - west) + (flow_y - south)) + (flow_z - under)
        source[pl.ds(pl.multiple_of(z * ROWS, ROWS), ROWS), cols] = value * (1.0 / DT)
        source[pl.ds(ROWS * LEVELS + z, 1), cols] = flow_x[ROWS - 1 :] * (-1.0 / DT)
        return carry

    lax.fori_loop(0, LEVELS * blocks, diverge, 0)

    def turning(b, carry):
        cols = pl.ds(pl.multiple_of(b * 256, 256), 256)
        high, low = split(source[:, cols])
        both = mxu(turn_t[...], high)
        turned[:, cols] = (both[:EXTRA] + both[EXTRA:]) + mxu(turn_t[pl.ds(0, EXTRA), :], low)
        return carry

    lax.fori_loop(0, blocks, turning, 0)
    load.wait()
    width = min(half, 256)
    for part in range(2):
        one = turned[:, pl.ds(0, half)]
        two = turned[:, pl.ds(half, half)]
        high, low = split(one + two if part == 0 else one - two)
        stacked = jnp.concatenate([high, low], axis=0)

        def transform(b, carry):
            cols = pl.ds(pl.multiple_of(b * width, width), width)
            both = mxu(stacked, y_t[2 * part, :, cols])
            value = (both[:EXTRA] + both[EXTRA:]) + mxu(high, y_t[2 * part + 1, :, cols])
            spectrum[:, pl.ds(pl.multiple_of(part * half + b * width, width), width)] = value
            return carry

        lax.fori_loop(0, half // width, transform, 0)

    def scans(t, carry):
        cols = pl.ds(pl.multiple_of(t * LANES, LANES), LANES)
        root = modes[0, :, cols]
        lead = spectrum[pl.ds(0, 8), cols]
        for x in range(1, ROWS + 1):
            lead = spectrum[pl.ds(8 * x, 8), cols] + root * lead
        trail = spectrum[pl.ds(8 * ROWS, 8), cols]
        for x in range(ROWS - 1, -1, -1):
            trail = spectrum[pl.ds(8 * x, 8), cols] + root * trail
        ends[t] = lead
        ends[tiles + t] = trail
        return carry

    lax.fori_loop(0, tiles, scans, 0)


def chain_kernel(ends, jump, dst, held, result, sems):
    me = lax.axis_index("gx")
    nest = lax.axis_index("nest")
    group = held.shape[0]
    count = ends.shape[0]
    tiles = count // 2
    mine = lax.rem(me, 2) == 0
    solver = me // 2

    def send(t, carry):
        @pl.when(2 * t != me)
        def _():
            remote(ends.at[t], held.at[me], sems.at[0], sems.at[1], nest, 2 * t).start()

        return carry

    lax.fori_loop(0, count, send, 0)

    @pl.when(mine)
    def _():
        pltpu.make_async_copy(ends.at[solver], held.at[me], sems.at[1]).start()
        back = solver >= tiles
        kind = jnp.where(back, solver - tiles, solver)
        ratio = jump[kind, 0]
        await_bytes(held, sems.at[1])

        def place(i):
            return jnp.where(back, group - 1 - i, i)

        def total(i, value):
            return value * ratio + held[place(i)]

        start = lax.fori_loop(0, group, total, jnp.zeros((8, LANES), f32)) * jump[kind, 1]

        def walk(i, value):
            g = place(i)
            result[g] = value

            @pl.when(g != me)
            def _():
                remote(result.at[g], dst.at[solver], sems.at[2], sems.at[3], nest, g).start()

            @pl.when(g == me)
            def _():
                pltpu.make_async_copy(result.at[g], dst.at[solver], sems.at[3]).start()

            return held[g] + ratio * value

        lax.fori_loop(0, group, walk, start)
        await_bytes(result.at[pl.ds(0, group - 1)], sems.at[2])
        await_bytes(ends.at[pl.ds(0, count - 1)], sems.at[0])

    @pl.when(jnp.logical_not(mine))
    def _():
        await_bytes(ends, sems.at[0])

    await_bytes(dst, sems.at[3])


def backward_kernel(
    coupled, spectrum, incoming, heights, back_t, modes, y_any,
    updated, pressure, y_t, waves, folded, east, sem,
):
    columns = coupled.shape[-1]
    half = columns // 2
    tiles = columns // LANES
    blocks = columns // 256
    load = pltpu.make_async_copy(y_any, y_t, sem)
    load.start()
    waves[pl.ds(8 * (ROWS + 1), 8), :] = jnp.zeros((8, columns), f32)

    def scans(t, carry):
        cols = pl.ds(pl.multiple_of(t * LANES, LANES), LANES)
        root = modes[0, :, cols]
        scale = modes[1, :, cols]
        trail = spectrum[pl.ds(8 * ROWS, 8), cols] + incoming[tiles + t]
        trails = [trail]
        for x in range(ROWS - 1, 0, -1):
            trail = spectrum[pl.ds(8 * x, 8), cols] + root * trail
            trails.append(trail)
        lead = incoming[t] + spectrum[pl.ds(0, 8), cols]
        for x in range(ROWS):
            if x:
                lead = spectrum[pl.ds(8 * x, 8), cols] + root * lead
            waves[pl.ds(8 * x, 8), cols] = (lead + root * trails[ROWS - 1 - x]) * scale
        waves[pl.ds(8 * ROWS, 8), cols] = (root * lead + trails[0]) * scale
        return carry

    lax.fori_loop(0, tiles, scans, 0)
    load.wait()
    width = min(half, 256)
    parts = []
    for part in range(2):
        high, low = split(waves[:, pl.ds(part * half, half)])
        parts.append((jnp.concatenate([high, low], axis=0), high))

    def transform(b, carry):
        cols = pl.ds(pl.multiple_of(b * width, width), width)
        values = []
        for part in range(2):
            stacked, high = parts[part]
            both = mxu(stacked, y_t[2 * part, :, cols])
            values.append((both[:EXTRA] + both[EXTRA:]) + mxu(high, y_t[2 * part + 1, :, cols]))
        folded[:, cols] = values[0] + values[1]
        folded[:, pl.ds(pl.multiple_of(half + b * width, width), width)] = values[0] - values[1]
        return carry

    lax.fori_loop(0, half // width, transform, 0)

    def turning(b, carry):
        cols = pl.ds(pl.multiple_of(b * 256, 256), 256)
        high, low = split(folded[:, cols])
        both = mxu(back_t[...], high)
        value = (both[:EXTRA] + both[EXTRA:]) + mxu(back_t[pl.ds(0, EXTRA), :], low)
        pressure[:, :, cols] = value[: ROWS * LEVELS].reshape(LEVELS, ROWS, 256)
        east[:, cols] = value[ROWS * LEVELS : ROWS * LEVELS + LEVELS]
        return carry

    lax.fori_loop(0, blocks, turning, 0)
    row = lax.broadcasted_iota(jnp.int32, (ROWS, 256), 0)

    def project(i, carry):
        z = i // blocks
        start = pl.multiple_of(lax.rem(i, blocks) * 256, 256)
        cols = pl.ds(start, 256)
        after = pl.ds(pl.multiple_of(lax.rem(start + 256, columns), LANES), LANES)
        own = pressure[z, :, cols]
        beyond = jnp.concatenate([own, pressure[z, :, after]], axis=1)
        north = pltpu.roll(beyond, 383, 1)[:, :256]
        plus = jnp.where(row == ROWS - 1, east[pl.ds(z, 1), cols], pltpu.roll(own, ROWS - 1, 0))
        top = pressure[jnp.minimum(z + 1, LEVELS - 1), :, cols]
        top = top * jnp.where(z < LEVELS - 1, 1.0, 0.0).astype(f32)
        mask = jnp.where(z >= heights[:, cols], 1.0, 0.0).astype(f32)
        updated[0, z, :, cols] = mask * (coupled[0, z, :, cols] - DT * (plus - own))
        updated[1, z, :, cols] = mask * (coupled[1, z, :, cols] - DT * (north - own))
        updated[2, z, :, cols] = mask * (coupled[2, z, :, cols] - DT * (top - own))
        return carry

    lax.fori_loop(0, LEVELS * blocks, project, 0)


def local(velocity, viscosity, heights, row_offset, column_offset):
    flow, viscous, roofs = velocity[0], viscosity[0], heights[0]
    columns = flow.shape[-1]
    group = lax.axis_size("gx")
    x_total = group * ROWS
    tiles = columns // LANES
    half = columns // 2
    t = {name: jnp.asarray(value) for name, value in tables(x_total, columns, group).items()}
    params = pltpu.CompilerParams(**PARAMS)
    effects = pltpu.CompilerParams(has_side_effects=True, **PARAMS)
    shape = lambda *dims: jax.ShapeDtypeStruct(dims, f32)
    vmem = pltpu.VMEM
    dma = pltpu.SemaphoreType.DMA

    west, east = pl.pallas_call(
        halo_kernel,
        out_shape=[shape(4, LEVELS, columns)] * 2,
        in_specs=[VMEM_SPEC] * 2,
        out_specs=[VMEM_SPEC] * 2,
        scratch_shapes=[vmem((2, 4, LEVELS, columns), f32), dma((4,))],
        compiler_params=effects,
        name="halo",
    )(flow, viscous)
    prov, chunks = pl.pallas_call(
        stencil_kernel,
        out_shape=[shape(3, LEVELS, ROWS, columns), shape(group, 3, ROWS, LANES)],
        in_specs=[SMEM_SPEC] + [VMEM_SPEC] * 6,
        out_specs=[VMEM_SPEC] * 2,
        scratch_shapes=[vmem((24 * 8, columns), f32), vmem((tiles, ROWS, LANES), f32)],
        compiler_params=params,
        name="stencil",
    )(column_offset, flow, viscous, roofs, west, east, t["pair"])
    under, above = pl.pallas_call(
        gather_kernel,
        out_shape=[shape(3, x_total + ROWS, LANES), shape(3, x_total // 2 + 3 * ROWS, LANES)],
        in_specs=[VMEM_SPEC],
        out_specs=[VMEM_SPEC] * 2,
        scratch_shapes=[dma((3,))],
        compiler_params=effects,
        name="gather",
    )(chunks)
    to_child, to_parent = pl.pallas_call(
        shift_kernel,
        out_shape=[shape(group, 32, LANES), shape(group, 48, LANES)],
        in_specs=[SMEM_SPEC] + [VMEM_SPEC] * 2,
        out_specs=[VMEM_SPEC] * 2,
        compiler_params=params,
        name="shift",
    )(row_offset, under, above)
    got = pl.pallas_call(
        scatter_kernel,
        out_shape=shape(group, 48, LANES),
        in_specs=[VMEM_SPEC] * 2,
        out_specs=VMEM_SPEC,
        scratch_shapes=[dma((3,))],
        compiler_params=effects,
        name="scatter",
    )(to_child, to_parent)
    coupled, spectrum, ends = pl.pallas_call(
        forward_kernel,
        out_shape=[shape(3, LEVELS, ROWS, columns), shape(EXTRA, columns), shape(2 * tiles, 8, LANES)],
        in_specs=[SMEM_SPEC] * 2 + [VMEM_SPEC] * 6 + [ANY_SPEC],
        out_specs=[VMEM_SPEC] * 3,
        scratch_shapes=[
            vmem((4, half, half), bf16),
            vmem((24, tiles, ROWS, LANES), f32),
            vmem((8, 32, columns), f32),
            vmem((ROWS, columns), f32),
            vmem((EXTRA, columns), f32),
            vmem((EXTRA, columns), f32),
            dma(()),
        ],
        compiler_params=params,
        name="forward",
    )(row_offset, column_offset, prov, got, roofs, t["wide"], t["turn"], t["modes"], t["y"])
    incoming = pl.pallas_call(
        chain_kernel,
        out_shape=shape(2 * tiles, 8, LANES),
        in_specs=[VMEM_SPEC] * 2,
        out_specs=VMEM_SPEC,
        scratch_shapes=[vmem((group, 8, LANES), f32), vmem((group, 8, LANES), f32), dma((4,))],
        compiler_params=effects,
        name="chain",
    )(ends, t["jump"])
    updated, pressure = pl.pallas_call(
        backward_kernel,
        out_shape=[shape(3, LEVELS, ROWS, columns), shape(LEVELS, ROWS, columns)],
        in_specs=[VMEM_SPEC] * 6 + [ANY_SPEC],
        out_specs=[VMEM_SPEC] * 2,
        scratch_shapes=[
            vmem((4, half, half), bf16),
            vmem((EXTRA, columns), f32),
            vmem((EXTRA, columns), f32),
            vmem((LEVELS, columns), f32),
            dma(()),
        ],
        compiler_params=params,
        name="backward",
    )(coupled, spectrum, incoming, roofs, t["back"], t["modes"], t["y"])
    return updated[None], pressure[None]


def solution(mesh):
    return jax.shard_map(
        local,
        mesh=mesh,
        in_specs=(
            P("nest", None, None, "gx", None),
            P("nest", None, "gx", None),
            P("nest", "gx", None),
            P(),
            P(),
        ),
        out_specs=(P("nest", None, None, "gx", None), P("nest", None, "gx", None)),
        check_vma=False,
    )
```

```python
import functools
import math

import jax
import jax.numpy as jnp
import ml_dtypes
import numpy as np
from jax import lax
from jax.experimental import pallas as pl
from jax.experimental.pallas import tpu as pltpu
from jax.sharding import PartitionSpec as P

LEVELS = 8
ROWS = 16
LANES = 128
EXTRA = 144
DT = 0.2
BLEND = 0.5
f32 = jnp.float32
bf16 = jnp.bfloat16
VMEM_SPEC = pl.BlockSpec(memory_space=pltpu.VMEM)
SMEM_SPEC = pl.BlockSpec(memory_space=pltpu.SMEM)
ANY_SPEC = pl.BlockSpec(memory_space=pl.ANY)
PARAMS = dict(vmem_limit_bytes=50 * 1024 * 1024)


def split_np(table):
    high = table.astype(ml_dtypes.bfloat16)
    low = (table - high.astype(np.float64)).astype(ml_dtypes.bfloat16)
    return high, low


def split(value):
    high = value.astype(bf16)
    low = (value - high.astype(f32)).astype(bf16)
    return high, low


def cas(angle):
    return np.cos(angle) + np.sin(angle)


@functools.lru_cache(maxsize=None)
def tables(x_total, columns, group):
    half = columns // 2
    m = np.arange(half)
    even = cas(2 * np.pi * ((m[:, None] * m[None, :]) % half) / half)
    odd_index = ((2 * m[:, None] + 1) * (2 * m[None, :] + 1)) % (2 * columns)
    odd = cas(2 * np.pi * odd_index / (2 * columns))
    even_high, even_low = split_np(even)
    odd_high, odd_low = split_np(odd)
    y_tables = np.stack([even_high, even_low, odd_high, odd_low])
    j = np.arange(LEVELS)
    z_vectors = math.sqrt(4 / 17) * np.cos((2 * j[:, None] + 1) * (2 * j[None, :] + 1) * np.pi / 34)
    z_values = 2 - 2 * np.cos((2 * j + 1) * np.pi / 17)
    turn = np.zeros((EXTRA, EXTRA))
    for x in range(ROWS + 1):
        for level in range(LEVELS):
            place = level * ROWS + x if x < ROWS else ROWS * LEVELS + level
            turn[x * LEVELS : x * LEVELS + LEVELS, place] = z_vectors[:, level]
    turn_high, turn_low = split_np(turn)
    back_high, back_low = split_np(turn.T)
    turn_stack = np.concatenate([turn_high, turn_low])
    back_stack = np.concatenate([back_high, back_low])
    wave = np.concatenate([2 * m, 2 * m + 1])
    mu = 4 * np.sin(np.pi * wave / columns)[None, :] ** 2 + z_values[:, None]
    root = 1 + mu / 2 - np.sqrt(mu + mu * mu / 4)
    scale = -1 / (1 / root - root) / columns
    modes = np.stack([root, scale]).astype(np.float32)
    reach = root**ROWS
    tiles = columns // LANES
    jump = np.stack([reach, 1 / (1 - reach**group)])
    jump = jump.reshape(2, LEVELS, tiles, LANES).transpose(2, 0, 1, 3).astype(np.float32)
    wide = np.zeros((2, 256, 256))
    for y in range(256):
        if y % 2 == 0:
            wide[:, y // 2, y] = 1
        else:
            wide[:, y // 2, y] = 0.5
            wide[0, y // 2 + 1, y] = 0.5
            wide[1, min(y // 2 + 1, 127), y] += 0.5
    pair = np.zeros((256, LANES))
    pair[np.arange(256), np.arange(256) // 2] = 0.5
    return dict(
        y=y_tables,
        turn=turn_stack,
        back=back_stack,
        modes=modes,
        jump=jump,
        wide=wide.astype(ml_dtypes.bfloat16),
        pair=pair.astype(ml_dtypes.bfloat16),
    )


def mxu(left, right):
    return jnp.dot(left, right, preferred_element_type=f32)


def greet(nest, k):
    pl.semaphore_signal(
        pltpu.get_barrier_semaphore(), inc=1, device_id={"nest": nest, "gx": k},
        device_id_type=pl.DeviceIdType.MESH,
    )


def halo_kernel(vel, visc, west, east, edge, sems):
    me = lax.axis_index("gx")
    nest = lax.axis_index("nest")
    group = lax.axis_size("gx")
    right = lax.rem(me + 1, group)
    left = lax.rem(me + group - 1, group)
    greet(nest, left)
    greet(nest, right)
    for c in range(3):
        edge[0, c] = vel[c, :, 0, :]
        edge[1, c] = vel[c, :, ROWS - 1, :]
    edge[0, 3] = visc[:, 0, :]
    edge[1, 3] = visc[:, ROWS - 1, :]
    pl.semaphore_wait(pltpu.get_barrier_semaphore(), 2)
    to_right = pltpu.make_async_remote_copy(
        edge.at[1], west, sems.at[0], sems.at[1], device_id={"gx": right},
        device_id_type=pl.DeviceIdType.MESH,
    )
    to_left = pltpu.make_async_remote_copy(
        edge.at[0], east, sems.at[2], sems.at[3], device_id={"gx": left},
        device_id_type=pl.DeviceIdType.MESH,
    )
    to_right.start()
    to_left.start()
    to_right.wait()
    to_left.wait()


def stencil_kernel(oy_ref, vel, visc, heights, west, east, pair, prov, out, mean, tile):
    columns = vel.shape[-1]
    tiles = columns // LANES
    blocks = columns // 256
    is_child = lax.axis_index("nest") == 1
    row = lax.broadcasted_iota(jnp.int32, (ROWS, 256), 0)
    lane = lax.broadcasted_iota(jnp.int32, (ROWS, LANES), 1)

    def cell(i, carry):
        z = i // blocks
        start = pl.multiple_of(lax.rem(i, blocks) * 256, 256)
        here = pl.ds(start, 256)
        before = pl.ds(pl.multiple_of(lax.rem(start + columns - LANES, columns), LANES), LANES)
        after = pl.ds(pl.multiple_of(lax.rem(start + 256, columns), LANES), LANES)
        up = jnp.minimum(z + 1, LEVELS - 1)
        down = jnp.maximum(z - 1, 0)
        up_open = jnp.where(z < LEVELS - 1, 1.0, 0.0).astype(f32)
        down_open = jnp.where(z > 0, 1.0, 0.0).astype(f32)

        def around(ref, lead, c):
            mid = ref[lead + (z, slice(None), here)]
            wide = jnp.concatenate(
                [ref[lead + (z, slice(None), before)], mid, ref[lead + (z, slice(None), after)]],
                axis=1,
            )
            north = pltpu.roll(wide, 511, 1)[:, LANES : LANES + 256]
            south = pltpu.roll(wide, 1, 1)[:, LANES : LANES + 256]
            plus = jnp.where(row == ROWS - 1, east[c, pl.ds(z, 1), here], pltpu.roll(mid, ROWS - 1, 0))
            minus = jnp.where(row == 0, west[c, pl.ds(z, 1), here], pltpu.roll(mid, 1, 0))
            top = ref[lead + (up, slice(None), here)]
            bottom = ref[lead + (down, slice(None), here)]
            return mid, plus, minus, north, south, top, bottom

        k, ke, kw, kn, ks, kt, kb = around(visc, (), 3)
        flow = [around(vel, (c,), c) for c in range(3)]
        half = 0.5 * DT
        kh = half * k
        b0, b1, b2 = (half * flow[c][0] for c in range(3))
        ae = (kh + half * ke) - b0
        aw = (kh + half * kw) + b0
        an = (kh + half * kn) - b1
        as_ = (kh + half * ks) + b1
        at = (kh + half * kt) - b2
        ab = (kh + half * kb) + b2
        mask = jnp.where(z >= heights[:, here], 1.0, 0.0).astype(f32)
        own = 1.0 - (((ae + aw) + (an + as_)) + (at + ab))
        at = at * up_open
        ab = ab * down_open
        for c in range(3):
            mid, plus, minus, north, south, top, bottom = flow[c]
            value = own * mid + ae * plus + aw * minus + an * north + as_ * south + at * top + ab * bottom
            prov[c, z, :, here] = value * mask
        return carry

    lax.fori_loop(0, LEVELS * blocks, cell, 0)

    @pl.when(jnp.logical_not(is_child))
    def _():
        oy = oy_ref[0]
        first = oy // LANES
        shift = lax.rem(oy, LANES)
        turn = lax.rem(LANES - shift, LANES)

        def unit(cz, carry):
            c = cz // LEVELS
            z = lax.rem(cz, LEVELS)
            moved = []
            for b in range(blocks + 1):
                cols = pl.ds(pl.multiple_of(lax.rem(first + b, tiles) * LANES, LANES), LANES)
                moved.append(pltpu.roll(prov[c, z, :, cols], turn, 1))
            for b in range(blocks):
                out[cz, :, pl.ds(b * LANES, LANES)] = jnp.where(lane < LANES - shift, moved[b], moved[b + 1])
            return carry

        lax.fori_loop(0, 24, unit, 0)

    @pl.when(is_child)
    def _():
        def rows(cz, carry):
            c = cz // LEVELS
            z = lax.rem(cz, LEVELS)
            for t in range(tiles):
                cols = pl.ds(t * LANES, LANES)
                tile[t] = prov[c, z, :, cols]
                evens = tile[t, pl.ds(0, 8, stride=2), :]
                odds = tile[t, pl.ds(1, 8, stride=2), :]
                mean[pl.ds(pl.multiple_of(cz * 8, 8), 8), cols] = 0.5 * (evens + odds)
            return carry

        lax.fori_loop(0, 24, rows, 0)
        for b in range(blocks):
            high, low = split(mean[:, pl.ds(b * 256, 256)])
            value = mxu(high, pair[...]) + mxu(low, pair[...])
            out[:, pl.ds(0, 8), pl.ds(b * LANES, LANES)] = value.reshape(24, 8, LANES)


def remote(src, dst, send, recv, nest, k):
    return pltpu.make_async_remote_copy(
        src, dst, send, recv, device_id={"nest": nest, "gx": k},
        device_id_type=pl.DeviceIdType.MESH,
    )


def await_bytes(ref, sem):
    pltpu.make_async_copy(ref, ref, sem).wait()


def align_kernel(src, beside, sems):
    me = lax.axis_index("gx")
    nest = lax.axis_index("nest")
    group = lax.axis_size("gx")
    step = jnp.where(nest == 0, group - 1, 1)
    target = lax.rem(me + step, group)
    greet(nest, lax.rem(me + group - step, group))
    pl.semaphore_wait(pltpu.get_barrier_semaphore(), 1)
    copy = remote(src.at[:, pl.ds(0, 8)], beside, sems.at[0], sems.at[1], nest, target)
    copy.start()
    copy.wait()


def shift_kernel(ox_ref, own, beside, even, odd):
    group = lax.axis_size("gx")
    half = own.shape[-1]
    me = lax.axis_index("gx")
    ox = ox_ref[0]
    rest = lax.rem(ox, 8)
    parity = lax.rem(ox // 8 + me, 2)

    @pl.when(lax.axis_index("nest") == 0)
    def _():
        def fill(i, carry):
            for b in range(half // LANES):
                cols = pl.ds(b * LANES, LANES)
                ninths = ([], [])
                for j in range(8):
                    cz = i * 8 + j
                    rows = jnp.concatenate([own[cz, :, cols], beside[cz, :, cols]], axis=0)
                    rows = pltpu.roll(rows, lax.rem(24 - rest, 24), 0)
                    place = pl.ds(pl.multiple_of(cz * 8, 8), 8)
                    even[place, cols] = rows[:8]
                    odd[place, cols] = rows[8:16]
                    ninths[0].append(rows[8:9])
                    ninths[1].append(rows[16:17])
                place = pl.ds(pl.multiple_of(192 + i * 8, 8), 8)
                even[place, cols] = jnp.concatenate(ninths[0], axis=0)
                odd[place, cols] = jnp.concatenate(ninths[1], axis=0)
            return carry

        lax.fori_loop(0, 3, fill, 0)

    @pl.when(lax.axis_index("nest") == 1)
    def _():
        mine = jnp.full((8, LANES), parity, jnp.int32) == 0

        def fill(cz, carry):
            place = pl.ds(pl.multiple_of(cz * 8, 8), 8)
            for b in range(half // LANES):
                cols = pl.ds(b * LANES, LANES)
                value = own[cz, pl.ds(0, 8), cols]
                rows = jnp.concatenate([value, beside[cz, :, cols]], axis=0)
                rows = pltpu.roll(rows, rest, 0)
                even[place, cols] = jnp.where(mine, rows[:8], rows[8:])
                odd[place, cols] = jnp.where(mine, rows[8:], rows[:8])
            return carry

        lax.fori_loop(0, 24, fill, 0)


def cross(shift, group, even, odd):
    pairs = ([], [])
    for g in range(group):
        block = shift + g
        pairs[block % 2].append((block // 2, group + g))
        pairs[block % 2].append((group + g, block // 2))
    if shift < group:
        pairs[shift % 2].append((2 * group - 1, (shift + group) // 2))
    axes = ("nest", "gx")
    return lax.ppermute(even, axes, pairs[0]), lax.ppermute(odd, axes, pairs[1])


def forward_kernel(
    ox_ref, oy_ref, prov, even, odd, heights, wide_t, turn_t, modes, y_any,
    coupled, spectrum, ends, y_t, mapped, wide, rate, source, turned, sem,
):
    columns = prov.shape[-1]
    group = lax.axis_size("gx")
    x_total = group * ROWS
    half = columns // 2
    tiles = columns // LANES
    blocks = columns // 256
    load = pltpu.make_async_copy(y_any, y_t, sem)
    load.start()
    me = lax.axis_index("gx")
    is_child = lax.axis_index("nest") == 1
    ox = ox_ref[0]
    oy = oy_ref[0]
    lane = lax.broadcasted_iota(jnp.int32, (ROWS, LANES), 1)
    row = lax.broadcasted_iota(jnp.int32, (ROWS, LANES), 0)

    @pl.when(is_child)
    def _():
        first_is_even = jnp.full((216, LANES), lax.rem(ox // 8 + me, 2), jnp.int32) == 0

        def block(b):
            cols = pl.ds(b * LANES, LANES)
            return jnp.where(first_is_even, even[:, cols], odd[:, cols])

        left = block(0)
        for b in range(blocks):
            right = block(min(b + 1, blocks - 1))
            high, low = split(jnp.concatenate([left, right], axis=1))
            table = wide_t[0 if b < blocks - 1 else 1]
            wide[:, pl.ds(b * 256, 256)] = mxu(high, table) + mxu(low, table)
            left = right
        tail = lax.broadcasted_iota(jnp.int32, (8, LANES), 0) == 7
        last = jnp.full((8, LANES), me, jnp.int32) == group - 1

        def unit(i, carry):
            for t in range(tiles):
                cols = pl.ds(t * LANES, LANES)
                ninths = wide[pl.ds(pl.multiple_of(192 + i * 8, 8), 8), cols]
                for j in range(8):
                    cz = i * 8 + j
                    own = wide[pl.ds(pl.multiple_of(cz * 8, 8), 8), cols]
                    ninth = jnp.where(last, own, ninths[j : j + 1])
                    after = jnp.where(tail, ninth, pltpu.roll(own, 7, 0))
                    mapped[cz, t, pl.ds(0, 8, stride=2), :] = own
                    mapped[cz, t, pl.ds(1, 8, stride=2), :] = 0.5 * (own + after)
            return carry

        lax.fori_loop(0, 3, unit, 0)

        def rates(t, carry):
            cols = pl.ds(pl.multiple_of(t * LANES, LANES), LANES)
            x = me * ROWS + row
            y = t * LANES + lane
            near_y = jnp.minimum(y, columns - 1 - y)
            near_x = jnp.minimum(x, x_total - 1 - x)
            near = jnp.minimum(near_x, near_y).astype(f32)
            rate[:, cols] = 0.2 + 0.8 * jnp.exp(-near * (16.0 / columns))
            return carry

        lax.fori_loop(0, tiles, rates, 0)

    @pl.when(jnp.logical_not(is_child))
    def _():
        first = oy // LANES
        shift = lax.rem(oy, LANES)

        def unit(cz, carry):
            rows = pl.ds(pl.multiple_of(cz * 8, 8), 8)
            moved = []
            for b in range(blocks):
                cols = pl.ds(b * LANES, LANES)
                both = jnp.concatenate([even[rows, cols], odd[rows, cols]], axis=0)
                moved.append(pltpu.roll(both, shift, 1))
            for b in range(blocks + 1):
                own = moved[min(b, blocks - 1)]
                before = moved[max(b - 1, 0)]
                mapped[cz, lax.rem(first + b, tiles)] = jnp.where(lane >= shift, own, before)
            return carry

        lax.fori_loop(0, 24, unit, 0)

        def rates(t, carry):
            cols = pl.ds(pl.multiple_of(t * LANES, LANES), LANES)
            x = me * ROWS + row
            y = t * LANES + lane
            j = y - oy
            j = jnp.where(j < 0, j + columns, j)
            inside = (x >= ox) & (x < ox + x_total // 2) & (j < half)
            rate[:, cols] = jnp.where(inside, BLEND, 0.0)
            return carry

        lax.fori_loop(0, tiles, rates, 0)

    source[pl.ds(ROWS * LEVELS, ROWS), :] = jnp.zeros((ROWS, columns), f32)

    def blend(i, carry):
        z = i // blocks
        b = lax.rem(i, blocks)
        cols = pl.ds(pl.multiple_of(b * 256, 256), 256)
        weight = rate[:, cols]
        mask = jnp.where(z >= heights[:, cols], 1.0, 0.0).astype(f32)
        for c in range(3):
            own = prov[c, z, :, cols]
            other = jnp.concatenate([mapped[c * LEVELS + z, 2 * b], mapped[c * LEVELS + z, 2 * b + 1]], axis=1)
            change = jnp.where(weight > 0.0, other - own, 0.0)
            coupled[c, z, :, cols] = (own + weight * change) * mask
        return carry

    lax.fori_loop(0, LEVELS * blocks, blend, 0)
    row2 = lax.broadcasted_iota(jnp.int32, (ROWS, 256), 0)

    def diverge(i, carry):
        z = i // blocks
        start = pl.multiple_of(lax.rem(i, blocks) * 256, 256)
        cols = pl.ds(start, 256)
        before = pl.ds(pl.multiple_of(lax.rem(start + columns - LANES, columns), LANES), LANES)
        flow_x = coupled[0, z, :, cols]
        flow_y = coupled[1, z, :, cols]
        flow_z = coupled[2, z, :, cols]
        beyond = jnp.concatenate([coupled[1, z, :, before], flow_y], axis=1)
        south = pltpu.roll(beyond, 1, 1)[:, LANES:]
        west = jnp.where(row2 == 0, 0.0, pltpu.roll(flow_x, 1, 0))
        under = coupled[2, jnp.maximum(z - 1, 0), :, cols] * jnp.where(z > 0, 1.0, 0.0).astype(f32)
        value = ((flow_x - west) + (flow_y - south)) + (flow_z - under)
        source[pl.ds(pl.multiple_of(z * ROWS, ROWS), ROWS), cols] = value * (1.0 / DT)
        source[pl.ds(ROWS * LEVELS + z, 1), cols] = flow_x[ROWS - 1 :] * (-1.0 / DT)
        return carry

    lax.fori_loop(0, LEVELS * blocks, diverge, 0)

    def turning(b, carry):
        cols = pl.ds(pl.multiple_of(b * 256, 256), 256)
        high, low = split(source[:, cols])
        both = mxu(turn_t[...], high)
        turned[:, cols] = (both[:EXTRA] + both[EXTRA:]) + mxu(turn_t[pl.ds(0, EXTRA), :], low)
        return carry

    lax.fori_loop(0, blocks, turning, 0)
    load.wait()
    width = min(half, 256)
    for part in range(2):
        one = turned[:, pl.ds(0, half)]
        two = turned[:, pl.ds(half, half)]
        high, low = split(one + two if part == 0 else one - two)
        stacked = jnp.concatenate([high, low], axis=0)

        def transform(b, carry):
            cols = pl.ds(pl.multiple_of(b * width, width), width)
            both = mxu(stacked, y_t[2 * part, :, cols])
            value = (both[:EXTRA] + both[EXTRA:]) + mxu(high, y_t[2 * part + 1, :, cols])
            spectrum[:, pl.ds(pl.multiple_of(part * half + b * width, width), width)] = value
            return carry

        lax.fori_loop(0, half // width, transform, 0)

    def scans(t, carry):
        cols = pl.ds(pl.multiple_of(t * LANES, LANES), LANES)
        root = modes[0, :, cols]
        lead = spectrum[pl.ds(0, 8), cols]
        for x in range(1, ROWS + 1):
            lead = spectrum[pl.ds(8 * x, 8), cols] + root * lead
        trail = spectrum[pl.ds(8 * ROWS, 8), cols]
        for x in range(ROWS - 1, -1, -1):
            trail = spectrum[pl.ds(8 * x, 8), cols] + root * trail
        ends[t] = lead
        ends[tiles + t] = trail
        return carry

    lax.fori_loop(0, tiles, scans, 0)


def chain_kernel(ends, jump, dst, held, result, sems):
    me = lax.axis_index("gx")
    nest = lax.axis_index("nest")
    group = held.shape[0]
    count = ends.shape[0]
    tiles = count // 2
    mine = lax.rem(me, 2) == 0
    solver = me // 2

    @pl.when(mine)
    def _():
        def hello(i, carry):
            greet(nest, lax.rem(me + i, group))
            return carry

        lax.fori_loop(1, group, hello, 0)
        pl.semaphore_wait(pltpu.get_barrier_semaphore(), group - 1)

    @pl.when(jnp.logical_not(mine))
    def _():
        def hello(i, carry):
            greet(nest, 2 * i)
            return carry

        lax.fori_loop(0, count, hello, 0)
        pl.semaphore_wait(pltpu.get_barrier_semaphore(), count)

    def send(t, carry):
        @pl.when(2 * t != me)
        def _():
            remote(ends.at[t], held.at[me], sems.at[0], sems.at[1], nest, 2 * t).start()

        return carry

    lax.fori_loop(0, count, send, 0)

    @pl.when(mine)
    def _():
        pltpu.make_async_copy(ends.at[solver], held.at[me], sems.at[1]).start()
        back = solver >= tiles
        kind = jnp.where(back, solver - tiles, solver)
        ratio = jump[kind, 0]
        await_bytes(held, sems.at[1])

        def place(i):
            return jnp.where(back, group - 1 - i, i)

        def total(i, value):
            return value * ratio + held[place(i)]

        start = lax.fori_loop(0, group, total, jnp.zeros((8, LANES), f32)) * jump[kind, 1]

        def walk(i, value):
            g = place(i)
            result[g] = value

            @pl.when(g != me)
            def _():
                remote(result.at[g], dst.at[solver], sems.at[2], sems.at[3], nest, g).start()

            @pl.when(g == me)
            def _():
                pltpu.make_async_copy(result.at[g], dst.at[solver], sems.at[3]).start()

            return held[g] + ratio * value

        lax.fori_loop(0, group, walk, start)
        await_bytes(result.at[pl.ds(0, group - 1)], sems.at[2])
        await_bytes(ends.at[pl.ds(0, count - 1)], sems.at[0])

    @pl.when(jnp.logical_not(mine))
    def _():
        await_bytes(ends, sems.at[0])

    await_bytes(dst, sems.at[3])


def backward_kernel(
    coupled, spectrum, incoming, heights, back_t, modes, y_any,
    updated, pressure, y_t, waves, folded, east, sem,
):
    columns = coupled.shape[-1]
    half = columns // 2
    tiles = columns // LANES
    blocks = columns // 256
    load = pltpu.make_async_copy(y_any, y_t, sem)
    load.start()
    waves[pl.ds(8 * (ROWS + 1), 8), :] = jnp.zeros((8, columns), f32)

    def scans(t, carry):
        cols = pl.ds(pl.multiple_of(t * LANES, LANES), LANES)
        root = modes[0, :, cols]
        scale = modes[1, :, cols]
        trail = spectrum[pl.ds(8 * ROWS, 8), cols] + incoming[tiles + t]
        trails = [trail]
        for x in range(ROWS - 1, 0, -1):
            trail = spectrum[pl.ds(8 * x, 8), cols] + root * trail
            trails.append(trail)
        lead = incoming[t] + spectrum[pl.ds(0, 8), cols]
        for x in range(ROWS):
            if x:
                lead = spectrum[pl.ds(8 * x, 8), cols] + root * lead
            waves[pl.ds(8 * x, 8), cols] = (lead + root * trails[ROWS - 1 - x]) * scale
        waves[pl.ds(8 * ROWS, 8), cols] = (root * lead + trails[0]) * scale
        return carry

    lax.fori_loop(0, tiles, scans, 0)
    load.wait()
    width = min(half, 256)
    parts = []
    for part in range(2):
        high, low = split(waves[:, pl.ds(part * half, half)])
        parts.append((jnp.concatenate([high, low], axis=0), high))

    def transform(b, carry):
        cols = pl.ds(pl.multiple_of(b * width, width), width)
        values = []
        for part in range(2):
            stacked, high = parts[part]
            both = mxu(stacked, y_t[2 * part, :, cols])
            values.append((both[:EXTRA] + both[EXTRA:]) + mxu(high, y_t[2 * part + 1, :, cols]))
        folded[:, cols] = values[0] + values[1]
        folded[:, pl.ds(pl.multiple_of(half + b * width, width), width)] = values[0] - values[1]
        return carry

    lax.fori_loop(0, half // width, transform, 0)

    def turning(b, carry):
        cols = pl.ds(pl.multiple_of(b * 256, 256), 256)
        high, low = split(folded[:, cols])
        both = mxu(back_t[...], high)
        value = (both[:EXTRA] + both[EXTRA:]) + mxu(back_t[pl.ds(0, EXTRA), :], low)
        pressure[:, :, cols] = value[: ROWS * LEVELS].reshape(LEVELS, ROWS, 256)
        east[:, cols] = value[ROWS * LEVELS : ROWS * LEVELS + LEVELS]
        return carry

    lax.fori_loop(0, blocks, turning, 0)
    row = lax.broadcasted_iota(jnp.int32, (ROWS, 256), 0)

    def project(i, carry):
        z = i // blocks
        start = pl.multiple_of(lax.rem(i, blocks) * 256, 256)
        cols = pl.ds(start, 256)
        after = pl.ds(pl.multiple_of(lax.rem(start + 256, columns), LANES), LANES)
        own = pressure[z, :, cols]
        beyond = jnp.concatenate([own, pressure[z, :, after]], axis=1)
        north = pltpu.roll(beyond, 383, 1)[:, :256]
        plus = jnp.where(row == ROWS - 1, east[pl.ds(z, 1), cols], pltpu.roll(own, ROWS - 1, 0))
        top = pressure[jnp.minimum(z + 1, LEVELS - 1), :, cols]
        top = top * jnp.where(z < LEVELS - 1, 1.0, 0.0).astype(f32)
        mask = jnp.where(z >= heights[:, cols], 1.0, 0.0).astype(f32)
        updated[0, z, :, cols] = mask * (coupled[0, z, :, cols] - DT * (plus - own))
        updated[1, z, :, cols] = mask * (coupled[1, z, :, cols] - DT * (north - own))
        updated[2, z, :, cols] = mask * (coupled[2, z, :, cols] - DT * (top - own))
        return carry

    lax.fori_loop(0, LEVELS * blocks, project, 0)


def local(velocity, viscosity, heights, row_offset, column_offset):
    flow, viscous, roofs = velocity[0], viscosity[0], heights[0]
    columns = flow.shape[-1]
    group = lax.axis_size("gx")
    x_total = group * ROWS
    tiles = columns // LANES
    half = columns // 2
    t = {name: jnp.asarray(value) for name, value in tables(x_total, columns, group).items()}
    params = pltpu.CompilerParams(**PARAMS)
    effects = lambda number: pltpu.CompilerParams(has_side_effects=True, collective_id=number, **PARAMS)
    shape = lambda *dims: jax.ShapeDtypeStruct(dims, f32)
    vmem = pltpu.VMEM
    dma = pltpu.SemaphoreType.DMA

    west, east = pl.pallas_call(
        halo_kernel,
        out_shape=[shape(4, LEVELS, columns)] * 2,
        in_specs=[VMEM_SPEC] * 2,
        out_specs=[VMEM_SPEC] * 2,
        scratch_shapes=[vmem((2, 4, LEVELS, columns), f32), dma((4,))],
        compiler_params=effects(0),
        name="halo",
    )(flow, viscous)
    prov, chunks = pl.pallas_call(
        stencil_kernel,
        out_shape=[shape(3, LEVELS, ROWS, columns), shape(24, ROWS, half)],
        in_specs=[SMEM_SPEC] + [VMEM_SPEC] * 6,
        out_specs=[VMEM_SPEC] * 2,
        scratch_shapes=[vmem((24 * 8, columns), f32), vmem((tiles, ROWS, LANES), f32)],
        compiler_params=params,
        name="stencil",
    )(column_offset, flow, viscous, roofs, west, east, t["pair"])
    beside = pl.pallas_call(
        align_kernel,
        out_shape=shape(24, 8, half),
        in_specs=[VMEM_SPEC],
        out_specs=VMEM_SPEC,
        scratch_shapes=[dma((2,))],
        compiler_params=effects(1),
        name="align",
    )(chunks)
    even, odd = pl.pallas_call(
        shift_kernel,
        out_shape=[shape(216, half)] * 2,
        in_specs=[SMEM_SPEC] + [VMEM_SPEC] * 2,
        out_specs=[VMEM_SPEC] * 2,
        compiler_params=params,
        name="shift",
    )(row_offset, chunks, beside)
    even, odd = lax.switch(
        row_offset[0] // 8,
        [functools.partial(cross, number, group) for number in range(group + 1)],
        even,
        odd,
    )
    coupled, spectrum, ends = pl.pallas_call(
        forward_kernel,
        out_shape=[shape(3, LEVELS, ROWS, columns), shape(EXTRA, columns), shape(2 * tiles, 8, LANES)],
        in_specs=[SMEM_SPEC] * 2 + [VMEM_SPEC] * 7 + [ANY_SPEC],
        out_specs=[VMEM_SPEC] * 3,
        scratch_shapes=[
            vmem((4, half, half), bf16),
            vmem((24, tiles, ROWS, LANES), f32),
            vmem((216, columns), f32),
            vmem((ROWS, columns), f32),
            vmem((EXTRA, columns), f32),
            vmem((EXTRA, columns), f32),
            dma(()),
        ],
        compiler_params=params,
        name="forward",
    )(row_offset, column_offset, prov, even, odd, roofs, t["wide"], t["turn"], t["modes"], t["y"])
    incoming = pl.pallas_call(
        chain_kernel,
        out_shape=shape(2 * tiles, 8, LANES),
        in_specs=[VMEM_SPEC] * 2,
        out_specs=VMEM_SPEC,
        scratch_shapes=[vmem((group, 8, LANES), f32), vmem((group, 8, LANES), f32), dma((4,))],
        compiler_params=effects(2),
        name="chain",
    )(ends, t["jump"])
    updated, pressure = pl.pallas_call(
        backward_kernel,
        out_shape=[shape(3, LEVELS, ROWS, columns), shape(LEVELS, ROWS, columns)],
        in_specs=[VMEM_SPEC] * 6 + [ANY_SPEC],
        out_specs=[VMEM_SPEC] * 2,
        scratch_shapes=[
            vmem((4, half, half), bf16),
            vmem((EXTRA, columns), f32),
            vmem((EXTRA, columns), f32),
            vmem((LEVELS, columns), f32),
            dma(()),
        ],
        compiler_params=params,
        name="backward",
    )(coupled, spectrum, incoming, roofs, t["back"], t["modes"], t["y"])
    return updated[None], pressure[None]


def solution(mesh):
    return jax.shard_map(
        local,
        mesh=mesh,
        in_specs=(
            P("nest", None, None, "gx", None),
            P("nest", None, "gx", None),
            P("nest", "gx", None),
            P(),
            P(),
        ),
        out_specs=(P("nest", None, None, "gx", None), P("nest", None, "gx", None)),
        check_vma=False,
    )
```

```python
import functools
import math

import jax
import jax.numpy as jnp
import ml_dtypes
import numpy as np
from jax import lax
from jax.experimental import pallas as pl
from jax.experimental.pallas import tpu as pltpu
from jax.sharding import PartitionSpec as P

LEVELS = 8
ROWS = 16
LANES = 128
EXTRA = 144
TEAM = 8
DT = 0.2
BLEND = 0.5
f32 = jnp.float32
bf16 = jnp.bfloat16
VMEM_SPEC = pl.BlockSpec(memory_space=pltpu.VMEM)
SMEM_SPEC = pl.BlockSpec(memory_space=pltpu.SMEM)
ANY_SPEC = pl.BlockSpec(memory_space=pl.ANY)
MIB = 1024 * 1024


def split_np(table):
    high = table.astype(ml_dtypes.bfloat16)
    low = (table - high.astype(np.float64)).astype(ml_dtypes.bfloat16)
    return high, low


def split(value):
    high = value.astype(bf16)
    low = (value - high.astype(f32)).astype(bf16)
    return high, low


def cas(angle):
    return np.cos(angle) + np.sin(angle)


@functools.lru_cache(maxsize=None)
def tables(x_total, columns, group):
    half = columns // 2
    m = np.arange(half)
    even = cas(2 * np.pi * ((m[:, None] * m[None, :]) % half) / half)
    odd_index = ((2 * m[:, None] + 1) * (2 * m[None, :] + 1)) % (2 * columns)
    odd = cas(2 * np.pi * odd_index / (2 * columns))
    even_high, even_low = split_np(even)
    odd_high, odd_low = split_np(odd)
    y_tables = np.stack([even_high, even_low, odd_high, odd_low])
    j = np.arange(LEVELS)
    z_vectors = math.sqrt(4 / 17) * np.cos((2 * j[:, None] + 1) * (2 * j[None, :] + 1) * np.pi / 34)
    z_values = 2 - 2 * np.cos((2 * j + 1) * np.pi / 17)
    turn = np.zeros((EXTRA, EXTRA))
    for x in range(ROWS + 1):
        for level in range(LEVELS):
            place = level * ROWS + x if x < ROWS else ROWS * LEVELS + level
            turn[x * LEVELS : x * LEVELS + LEVELS, place] = z_vectors[:, level]
    turn_high, turn_low = split_np(turn)
    back_high, back_low = split_np(turn.T)
    turn_stack = np.concatenate([turn_high, turn_low])
    back_stack = np.concatenate([back_high, back_low])
    wave = np.concatenate([2 * m, 2 * m + 1])
    mu = 4 * np.sin(np.pi * wave / columns)[None, :] ** 2 + z_values[:, None]
    root = 1 + mu / 2 - np.sqrt(mu + mu * mu / 4)
    scale = -1 / (1 / root - root) / columns
    modes = np.stack([root, scale]).astype(np.float32)
    reach = root**ROWS
    tiles = columns // LANES
    jump = np.stack([reach, reach**TEAM, 1 / (1 - reach**group)])
    jump = jump.reshape(3, LEVELS, tiles, LANES).transpose(0, 2, 1, 3).astype(np.float32)
    wide = np.zeros((2, 256, 256))
    for y in range(256):
        if y % 2 == 0:
            wide[:, y // 2, y] = 1
        else:
            wide[:, y // 2, y] = 0.5
            wide[0, y // 2 + 1, y] = 0.5
            wide[1, min(y // 2 + 1, 127), y] += 0.5
    pair = np.zeros((256, LANES))
    pair[np.arange(256), np.arange(256) // 2] = 0.5
    return dict(
        y=y_tables,
        turn=turn_stack,
        back=back_stack,
        modes=modes,
        jump=jump,
        wide=wide.astype(ml_dtypes.bfloat16),
        pair=pair.astype(ml_dtypes.bfloat16),
    )


def mxu(left, right):
    return jnp.dot(left, right, preferred_element_type=f32)


def greet(nest, k):
    pl.semaphore_signal(
        pltpu.get_barrier_semaphore(), inc=1, device_id={"nest": nest, "gx": k},
        device_id_type=pl.DeviceIdType.MESH,
    )


def halo_kernel(vel_any, visc_any, west, east, vel, visc, edge, sems):
    me = lax.axis_index("gx")
    nest = lax.axis_index("nest")
    group = lax.axis_size("gx")
    right = lax.rem(me + 1, group)
    left = lax.rem(me + group - 1, group)
    greet(nest, left)
    greet(nest, right)
    loads = [pltpu.make_async_copy(vel_any.at[c], vel.at[c], sems.at[4 + c]) for c in range(3)]
    loads.append(pltpu.make_async_copy(visc_any, visc, sems.at[7]))
    for load in loads:
        load.start()
    for load in loads:
        load.wait()
    for c in range(3):
        edge[0, c] = vel[c, :, 0, :]
        edge[1, c] = vel[c, :, ROWS - 1, :]
    edge[0, 3] = visc[:, 0, :]
    edge[1, 3] = visc[:, ROWS - 1, :]
    pl.semaphore_wait(pltpu.get_barrier_semaphore(), 2)
    to_right = pltpu.make_async_remote_copy(
        edge.at[1], west, sems.at[0], sems.at[1], device_id={"gx": right},
        device_id_type=pl.DeviceIdType.MESH,
    )
    to_left = pltpu.make_async_remote_copy(
        edge.at[0], east, sems.at[2], sems.at[3], device_id={"gx": left},
        device_id_type=pl.DeviceIdType.MESH,
    )
    to_right.start()
    to_left.start()
    to_right.wait()
    to_left.wait()


def stencil_kernel(oy_ref, vel, visc, heights, west, east, pair, prov, out, mean, tile):
    columns = vel.shape[-1]
    tiles = columns // LANES
    blocks = columns // 256
    is_child = lax.axis_index("nest") == 1
    row = lax.broadcasted_iota(jnp.int32, (ROWS, 256), 0)
    lane = lax.broadcasted_iota(jnp.int32, (ROWS, LANES), 1)

    def cell(i, carry):
        z = i // blocks
        start = pl.multiple_of(lax.rem(i, blocks) * 256, 256)
        here = pl.ds(start, 256)
        before = pl.ds(pl.multiple_of(lax.rem(start + columns - LANES, columns), LANES), LANES)
        after = pl.ds(pl.multiple_of(lax.rem(start + 256, columns), LANES), LANES)
        up = jnp.minimum(z + 1, LEVELS - 1)
        down = jnp.maximum(z - 1, 0)
        up_open = jnp.where(z < LEVELS - 1, 1.0, 0.0).astype(f32)
        down_open = jnp.where(z > 0, 1.0, 0.0).astype(f32)

        def around(ref, lead, c):
            mid = ref[lead + (z, slice(None), here)]
            wide = jnp.concatenate(
                [ref[lead + (z, slice(None), before)], mid, ref[lead + (z, slice(None), after)]],
                axis=1,
            )
            north = pltpu.roll(wide, 511, 1)[:, LANES : LANES + 256]
            south = pltpu.roll(wide, 1, 1)[:, LANES : LANES + 256]
            plus = jnp.where(row == ROWS - 1, east[c, pl.ds(z, 1), here], pltpu.roll(mid, ROWS - 1, 0))
            minus = jnp.where(row == 0, west[c, pl.ds(z, 1), here], pltpu.roll(mid, 1, 0))
            top = ref[lead + (up, slice(None), here)]
            bottom = ref[lead + (down, slice(None), here)]
            return mid, plus, minus, north, south, top, bottom

        k, ke, kw, kn, ks, kt, kb = around(visc, (), 3)
        flow = [around(vel, (c,), c) for c in range(3)]
        half = 0.5 * DT
        kh = half * k
        b0, b1, b2 = (half * flow[c][0] for c in range(3))
        ae = (kh + half * ke) - b0
        aw = (kh + half * kw) + b0
        an = (kh + half * kn) - b1
        as_ = (kh + half * ks) + b1
        at = (kh + half * kt) - b2
        ab = (kh + half * kb) + b2
        mask = jnp.where(z >= heights[:, here], 1.0, 0.0).astype(f32)
        own = 1.0 - (((ae + aw) + (an + as_)) + (at + ab))
        at = at * up_open
        ab = ab * down_open
        for c in range(3):
            mid, plus, minus, north, south, top, bottom = flow[c]
            value = own * mid + ae * plus + aw * minus + an * north + as_ * south + at * top + ab * bottom
            prov[c, z, :, here] = value * mask
        return carry

    lax.fori_loop(0, LEVELS * blocks, cell, 0)

    @pl.when(jnp.logical_not(is_child))
    def _():
        oy = oy_ref[0]
        first = oy // LANES
        shift = lax.rem(oy, LANES)
        turn = lax.rem(LANES - shift, LANES)

        def unit(cz, carry):
            c = cz // LEVELS
            z = lax.rem(cz, LEVELS)
            moved = []
            for b in range(blocks + 1):
                cols = pl.ds(pl.multiple_of(lax.rem(first + b, tiles) * LANES, LANES), LANES)
                moved.append(pltpu.roll(prov[c, z, :, cols], turn, 1))
            for b in range(blocks):
                out[cz, :, pl.ds(b * LANES, LANES)] = jnp.where(lane < LANES - shift, moved[b], moved[b + 1])
            return carry

        lax.fori_loop(0, 24, unit, 0)

    @pl.when(is_child)
    def _():
        def rows(cz, carry):
            c = cz // LEVELS
            z = lax.rem(cz, LEVELS)
            for t in range(tiles):
                cols = pl.ds(t * LANES, LANES)
                tile[t] = prov[c, z, :, cols]
                evens = tile[t, pl.ds(0, 8, stride=2), :]
                odds = tile[t, pl.ds(1, 8, stride=2), :]
                mean[pl.ds(pl.multiple_of(cz * 8, 8), 8), cols] = 0.5 * (evens + odds)
            return carry

        lax.fori_loop(0, 24, rows, 0)
        for b in range(blocks):
            high, low = split(mean[:, pl.ds(b * 256, 256)])
            value = mxu(high, pair[...]) + mxu(low, pair[...])
            out[:, pl.ds(0, 8), pl.ds(b * LANES, LANES)] = value.reshape(24, 8, LANES)


def remote(src, dst, send, recv, nest, k):
    return pltpu.make_async_remote_copy(
        src, dst, send, recv, device_id={"nest": nest, "gx": k},
        device_id_type=pl.DeviceIdType.MESH,
    )


def await_bytes(ref, sem):
    pltpu.make_async_copy(ref, ref, sem).wait()


def align_kernel(src, beside, sems):
    me = lax.axis_index("gx")
    nest = lax.axis_index("nest")
    group = lax.axis_size("gx")
    step = jnp.where(nest == 0, group - 1, 1)
    target = lax.rem(me + step, group)
    greet(nest, lax.rem(me + group - step, group))
    pl.semaphore_wait(pltpu.get_barrier_semaphore(), 1)
    copy = remote(src.at[:, pl.ds(0, 8)], beside, sems.at[0], sems.at[1], nest, target)
    copy.start()
    copy.wait()


def shift_kernel(ox_ref, own, beside, even, odd):
    group = lax.axis_size("gx")
    half = own.shape[-1]
    me = lax.axis_index("gx")
    ox = ox_ref[0]
    rest = lax.rem(ox, 8)
    parity = lax.rem(ox // 8 + me, 2)

    @pl.when(lax.axis_index("nest") == 0)
    def _():
        def fill(i, carry):
            for b in range(half // LANES):
                cols = pl.ds(b * LANES, LANES)
                ninths = ([], [])
                for j in range(8):
                    cz = i * 8 + j
                    rows = jnp.concatenate([own[cz, :, cols], beside[cz, :, cols]], axis=0)
                    rows = pltpu.roll(rows, lax.rem(24 - rest, 24), 0)
                    place = pl.ds(pl.multiple_of(cz * 8, 8), 8)
                    even[place, cols] = rows[:8]
                    odd[place, cols] = rows[8:16]
                    ninths[0].append(rows[8:9])
                    ninths[1].append(rows[16:17])
                place = pl.ds(pl.multiple_of(192 + i * 8, 8), 8)
                even[place, cols] = jnp.concatenate(ninths[0], axis=0)
                odd[place, cols] = jnp.concatenate(ninths[1], axis=0)
            return carry

        lax.fori_loop(0, 3, fill, 0)

    @pl.when(lax.axis_index("nest") == 1)
    def _():
        mine = jnp.full((8, LANES), parity, jnp.int32) == 0

        def fill(cz, carry):
            place = pl.ds(pl.multiple_of(cz * 8, 8), 8)
            for b in range(half // LANES):
                cols = pl.ds(b * LANES, LANES)
                value = own[cz, pl.ds(0, 8), cols]
                rows = jnp.concatenate([value, beside[cz, :, cols]], axis=0)
                rows = pltpu.roll(rows, rest, 0)
                even[place, cols] = jnp.where(mine, rows[:8], rows[8:])
                odd[place, cols] = jnp.where(mine, rows[8:], rows[:8])
            return carry

        lax.fori_loop(0, 24, fill, 0)


def cross_kernel(shift, even, odd, even_in, odd_in, sems):
    group = lax.axis_size("gx")
    me = lax.axis_index("gx")
    nest = lax.axis_index("nest")
    barrier = pltpu.get_barrier_semaphore()
    sources = (even, odd)
    targets = (even_in, odd_in)
    means = pl.ds(0, 192)
    last = group - 1
    spill = shift < group

    def greet_nest(other, k):
        pl.semaphore_signal(
            barrier, inc=1, device_id={"nest": other, "gx": k}, device_id_type=pl.DeviceIdType.MESH
        )

    @pl.when(nest == 0)
    def _():
        for e in range(2):
            g = 2 * me + e - shift

            @pl.when((g >= 0) & (g < group))
            def _():
                greet_nest(1, g)

            if spill:
                @pl.when(g == group)
                def _():
                    greet_nest(1, last)

        count = jnp.int32(0)
        for e in range(2):
            g = 2 * me + e - shift
            count = count + jnp.where((g >= 0) & (g < group), 1, 0)

        @pl.when(count > 0)
        def _():
            pl.semaphore_wait(barrier, count)

        for e in range(2):
            g = 2 * me + e - shift

            @pl.when((g >= 0) & (g < group))
            def _():
                remote(sources[e], targets[e], sems.at[0, e], sems.at[1, e], 1, g).start()

        for e in range(2):
            g = 2 * me + e - shift
            take = (g >= 0) & (g < group)

            @pl.when(take)
            def _():
                await_bytes(sources[e], sems.at[0, e])

            @pl.when(take | (g == group) if spill else take)
            def _():
                await_bytes(targets[e].at[means], sems.at[1, e])

    @pl.when(nest == 1)
    def _():
        block = shift + me
        q = block // 2
        e_mine = lax.rem(block, 2)
        greet_nest(0, q)
        pl.semaphore_wait(barrier, jnp.where(me == last, 2, 1) if spill else 1)
        if spill:
            @pl.when(me == last)
            def _():
                e = shift % 2
                k = (shift + group) // 2
                remote(sources[e].at[means], targets[e].at[means], sems.at[0, e], sems.at[1, e], 0, k).start()

        for e in range(2):
            @pl.when(e_mine == e)
            def _():
                remote(sources[e].at[means], targets[e].at[means], sems.at[0, e], sems.at[1, e], 0, q).start()

        for e in range(2):
            @pl.when(e_mine == e)
            def _():
                await_bytes(sources[e].at[means], sems.at[0, e])
                await_bytes(targets[e], sems.at[1, e])

        if spill:
            @pl.when(me == last)
            def _():
                await_bytes(sources[shift % 2].at[means], sems.at[0, shift % 2])


def cross(shift, params, even, odd):
    return pl.pallas_call(
        functools.partial(cross_kernel, shift),
        out_shape=[jax.ShapeDtypeStruct(even.shape, f32)] * 2,
        in_specs=[VMEM_SPEC] * 2,
        out_specs=[VMEM_SPEC] * 2,
        scratch_shapes=[pltpu.SemaphoreType.DMA((2, 2))],
        compiler_params=params,
        name="cross",
    )(even, odd)


def forward_kernel(
    ox_ref, oy_ref, prov, even, odd, heights, wide_t, turn_t, modes, y_any,
    coupled, spectrum, ends, y_t, mapped, wide, rate, source, turned, sems,
):
    columns = prov.shape[-1]
    loads = [pltpu.make_async_copy(y_any.at[i], y_t.at[i], sems.at[i]) for i in range(4)]
    for load in loads:
        load.start()
    group = lax.axis_size("gx")
    x_total = group * ROWS
    half = columns // 2
    tiles = columns // LANES
    blocks = columns // 256
    me = lax.axis_index("gx")
    is_child = lax.axis_index("nest") == 1
    ox = ox_ref[0]
    oy = oy_ref[0]
    lane = lax.broadcasted_iota(jnp.int32, (ROWS, LANES), 1)
    row = lax.broadcasted_iota(jnp.int32, (ROWS, LANES), 0)

    @pl.when(is_child)
    def _():
        first_is_even = jnp.full((216, LANES), lax.rem(ox // 8 + me, 2), jnp.int32) == 0

        def block(b):
            cols = pl.ds(b * LANES, LANES)
            return jnp.where(first_is_even, even[:, cols], odd[:, cols])

        left = block(0)
        for b in range(blocks):
            right = block(min(b + 1, blocks - 1))
            high, low = split(jnp.concatenate([left, right], axis=1))
            table = wide_t[0 if b < blocks - 1 else 1]
            wide[:, pl.ds(b * 256, 256)] = mxu(high, table) + mxu(low, table)
            left = right
        tail = lax.broadcasted_iota(jnp.int32, (8, LANES), 0) == 7
        last = jnp.full((8, LANES), me, jnp.int32) == group - 1

        def unit(i, carry):
            for t in range(tiles):
                cols = pl.ds(t * LANES, LANES)
                ninths = wide[pl.ds(pl.multiple_of(192 + i * 8, 8), 8), cols]
                for j in range(8):
                    cz = i * 8 + j
                    own = wide[pl.ds(pl.multiple_of(cz * 8, 8), 8), cols]
                    ninth = jnp.where(last, own, ninths[j : j + 1])
                    after = jnp.where(tail, ninth, pltpu.roll(own, 7, 0))
                    mapped[cz, t, pl.ds(0, 8, stride=2), :] = own
                    mapped[cz, t, pl.ds(1, 8, stride=2), :] = 0.5 * (own + after)
            return carry

        lax.fori_loop(0, 3, unit, 0)

        def rates(t, carry):
            cols = pl.ds(pl.multiple_of(t * LANES, LANES), LANES)
            x = me * ROWS + row
            y = t * LANES + lane
            near_y = jnp.minimum(y, columns - 1 - y)
            near_x = jnp.minimum(x, x_total - 1 - x)
            near = jnp.minimum(near_x, near_y).astype(f32)
            rate[:, cols] = 0.2 + 0.8 * jnp.exp(-near * (16.0 / columns))
            return carry

        lax.fori_loop(0, tiles, rates, 0)

    @pl.when(jnp.logical_not(is_child))
    def _():
        first = oy // LANES
        shift = lax.rem(oy, LANES)

        def unit(cz, carry):
            rows = pl.ds(pl.multiple_of(cz * 8, 8), 8)
            moved = []
            for b in range(blocks):
                cols = pl.ds(b * LANES, LANES)
                both = jnp.concatenate([even[rows, cols], odd[rows, cols]], axis=0)
                moved.append(pltpu.roll(both, shift, 1))
            for b in range(blocks + 1):
                own = moved[min(b, blocks - 1)]
                before = moved[max(b - 1, 0)]
                mapped[cz, lax.rem(first + b, tiles)] = jnp.where(lane >= shift, own, before)
            return carry

        lax.fori_loop(0, 24, unit, 0)

        def rates(t, carry):
            cols = pl.ds(pl.multiple_of(t * LANES, LANES), LANES)
            x = me * ROWS + row
            y = t * LANES + lane
            j = y - oy
            j = jnp.where(j < 0, j + columns, j)
            inside = (x >= ox) & (x < ox + x_total // 2) & (j < half)
            rate[:, cols] = jnp.where(inside, BLEND, 0.0)
            return carry

        lax.fori_loop(0, tiles, rates, 0)

    source[pl.ds(ROWS * LEVELS, ROWS), :] = jnp.zeros((ROWS, columns), f32)

    def blend(i, carry):
        z = i // blocks
        b = lax.rem(i, blocks)
        cols = pl.ds(pl.multiple_of(b * 256, 256), 256)
        weight = rate[:, cols]
        mask = jnp.where(z >= heights[:, cols], 1.0, 0.0).astype(f32)
        for c in range(3):
            own = prov[c, z, :, cols]
            other = jnp.concatenate([mapped[c * LEVELS + z, 2 * b], mapped[c * LEVELS + z, 2 * b + 1]], axis=1)
            change = jnp.where(weight > 0.0, other - own, 0.0)
            coupled[c, z, :, cols] = (own + weight * change) * mask
        return carry

    lax.fori_loop(0, LEVELS * blocks, blend, 0)
    row2 = lax.broadcasted_iota(jnp.int32, (ROWS, 256), 0)

    def diverge(i, carry):
        z = i // blocks
        start = pl.multiple_of(lax.rem(i, blocks) * 256, 256)
        cols = pl.ds(start, 256)
        before = pl.ds(pl.multiple_of(lax.rem(start + columns - LANES, columns), LANES), LANES)
        flow_x = coupled[0, z, :, cols]
        flow_y = coupled[1, z, :, cols]
        flow_z = coupled[2, z, :, cols]
        beyond = jnp.concatenate([coupled[1, z, :, before], flow_y], axis=1)
        south = pltpu.roll(beyond, 1, 1)[:, LANES:]
        west = jnp.where(row2 == 0, 0.0, pltpu.roll(flow_x, 1, 0))
        under = coupled[2, jnp.maximum(z - 1, 0), :, cols] * jnp.where(z > 0, 1.0, 0.0).astype(f32)
        value = ((flow_x - west) + (flow_y - south)) + (flow_z - under)
        source[pl.ds(pl.multiple_of(z * ROWS, ROWS), ROWS), cols] = value * (1.0 / DT)
        source[pl.ds(ROWS * LEVELS + z, 1), cols] = flow_x[ROWS - 1 :] * (-1.0 / DT)
        return carry

    lax.fori_loop(0, LEVELS * blocks, diverge, 0)

    def turning(b, carry):
        cols = pl.ds(pl.multiple_of(b * 256, 256), 256)
        high, low = split(source[:, cols])
        both = mxu(turn_t[...], high)
        turned[:, cols] = (both[:EXTRA] + both[EXTRA:]) + mxu(turn_t[pl.ds(0, EXTRA), :], low)
        return carry

    lax.fori_loop(0, blocks, turning, 0)
    for load in loads:
        load.wait()
    width = min(half, 256)
    for part in range(2):
        one = turned[:, pl.ds(0, half)]
        two = turned[:, pl.ds(half, half)]
        high, low = split(one + two if part == 0 else one - two)
        stacked = jnp.concatenate([high, low], axis=0)

        def transform(b, carry):
            cols = pl.ds(pl.multiple_of(b * width, width), width)
            both = mxu(stacked, y_t[2 * part, :, cols])
            value = (both[:EXTRA] + both[EXTRA:]) + mxu(high, y_t[2 * part + 1, :, cols])
            spectrum[:, pl.ds(pl.multiple_of(part * half + b * width, width), width)] = value
            return carry

        lax.fori_loop(0, half // width, transform, 0)

    def scans(t, carry):
        cols = pl.ds(pl.multiple_of(t * LANES, LANES), LANES)
        root = modes[0, :, cols]
        lead = spectrum[pl.ds(0, 8), cols]
        for x in range(1, ROWS + 1):
            lead = spectrum[pl.ds(8 * x, 8), cols] + root * lead
        trail = spectrum[pl.ds(8 * ROWS, 8), cols]
        for x in range(ROWS - 1, -1, -1):
            trail = spectrum[pl.ds(8 * x, 8), cols] + root * trail
        ends[t] = lead
        ends[tiles + t] = trail
        return carry

    lax.fori_loop(0, tiles, scans, 0)


def chain_kernel(ends, jump, dst, held, sums, result, sems):
    me = lax.axis_index("gx")
    nest = lax.axis_index("nest")
    size, share = ends.shape[:2]
    teams = sums.shape[0]
    tiles = jump.shape[1]
    team = me // size
    seat = lax.rem(me, size)
    near = [team * size + lax.rem(seat + i, size) for i in range(1, size)]
    far = [lax.rem(team + i, teams) * size + seat for i in range(1, teams)]
    for k in near + far:
        greet(nest, k)
    pl.semaphore_wait(pltpu.get_barrier_semaphore(), len(near) + len(far))
    for i in range(1, size):
        other = lax.rem(seat + i, size)
        remote(ends.at[other], held.at[seat], sems.at[0], sems.at[1], nest, team * size + other).start()
    held[seat] = ends[seat]
    first = seat * share
    back = first >= tiles
    own = pl.ds(jnp.where(back, first - tiles, first), share)
    ratio = jump[0, own]
    await_bytes(held.at[pl.ds(0, size - 1)], sems.at[1])

    def place(i):
        return jnp.where(back, size - 1 - i, i)

    total = held[place(0)]
    for i in range(1, size):
        total = total * ratio + held[place(i)]
    sums[team] = total
    for i in range(1, teams):
        k = lax.rem(team + i, teams) * size + seat
        remote(sums.at[team], sums.at[team], sems.at[2], sems.at[3], nest, k).start()
    await_bytes(sums.at[pl.ds(0, teams - 1)], sems.at[3])
    value = total
    for i in range(1, teams):
        at = jnp.where(back, lax.rem(team + teams - i, teams), lax.rem(team + i, teams))
        value = value * jump[1, own] + sums[at]
    value = value * jump[2, own]
    for i in range(size):
        g = place(i)
        result[g] = value
        if i < size - 1:
            value = held[g] + ratio * value
    for i in range(1, size):
        other = lax.rem(seat + i, size)
        remote(result.at[other], dst.at[seat], sems.at[4], sems.at[5], nest, team * size + other).start()
    dst[seat] = result[seat]
    await_bytes(ends.at[pl.ds(0, size - 1)], sems.at[0])
    await_bytes(sums.at[pl.ds(0, teams - 1)], sems.at[2])
    await_bytes(result.at[pl.ds(0, size - 1)], sems.at[4])
    await_bytes(dst.at[pl.ds(0, size - 1)], sems.at[5])


def backward_kernel(
    coupled, spectrum, incoming, heights, back_t, modes, y_t,
    updated, pressure, waves, folded, east,
):
    columns = coupled.shape[-1]
    half = columns // 2
    tiles = columns // LANES
    blocks = columns // 256
    waves[pl.ds(8 * (ROWS + 1), 8), :] = jnp.zeros((8, columns), f32)

    def scans(t, carry):
        cols = pl.ds(pl.multiple_of(t * LANES, LANES), LANES)
        root = modes[0, :, cols]
        scale = modes[1, :, cols]
        trail = spectrum[pl.ds(8 * ROWS, 8), cols] + incoming[tiles + t]
        trails = [trail]
        for x in range(ROWS - 1, 0, -1):
            trail = spectrum[pl.ds(8 * x, 8), cols] + root * trail
            trails.append(trail)
        lead = incoming[t] + spectrum[pl.ds(0, 8), cols]
        for x in range(ROWS):
            if x:
                lead = spectrum[pl.ds(8 * x, 8), cols] + root * lead
            waves[pl.ds(8 * x, 8), cols] = (lead + root * trails[ROWS - 1 - x]) * scale
        waves[pl.ds(8 * ROWS, 8), cols] = (root * lead + trails[0]) * scale
        return carry

    lax.fori_loop(0, tiles, scans, 0)
    width = min(half, 256)
    parts = []
    for part in range(2):
        high, low = split(waves[:, pl.ds(part * half, half)])
        parts.append((jnp.concatenate([high, low], axis=0), high))

    def transform(b, carry):
        cols = pl.ds(pl.multiple_of(b * width, width), width)
        values = []
        for part in range(2):
            stacked, high = parts[part]
            both = mxu(stacked, y_t[2 * part, :, cols])
            values.append((both[:EXTRA] + both[EXTRA:]) + mxu(high, y_t[2 * part + 1, :, cols]))
        folded[:, cols] = values[0] + values[1]
        folded[:, pl.ds(pl.multiple_of(half + b * width, width), width)] = values[0] - values[1]
        return carry

    lax.fori_loop(0, half // width, transform, 0)

    def turning(b, carry):
        cols = pl.ds(pl.multiple_of(b * 256, 256), 256)
        high, low = split(folded[:, cols])
        both = mxu(back_t[...], high)
        value = (both[:EXTRA] + both[EXTRA:]) + mxu(back_t[pl.ds(0, EXTRA), :], low)
        pressure[:, :, cols] = value[: ROWS * LEVELS].reshape(LEVELS, ROWS, 256)
        east[:, cols] = value[ROWS * LEVELS : ROWS * LEVELS + LEVELS]
        return carry

    lax.fori_loop(0, blocks, turning, 0)
    row = lax.broadcasted_iota(jnp.int32, (ROWS, 256), 0)

    def project(i, carry):
        z = i // blocks
        start = pl.multiple_of(lax.rem(i, blocks) * 256, 256)
        cols = pl.ds(start, 256)
        after = pl.ds(pl.multiple_of(lax.rem(start + 256, columns), LANES), LANES)
        own = pressure[z, :, cols]
        beyond = jnp.concatenate([own, pressure[z, :, after]], axis=1)
        north = pltpu.roll(beyond, 383, 1)[:, :256]
        plus = jnp.where(row == ROWS - 1, east[pl.ds(z, 1), cols], pltpu.roll(own, ROWS - 1, 0))
        top = pressure[jnp.minimum(z + 1, LEVELS - 1), :, cols]
        top = top * jnp.where(z < LEVELS - 1, 1.0, 0.0).astype(f32)
        mask = jnp.where(z >= heights[:, cols], 1.0, 0.0).astype(f32)
        updated[0, z, :, cols] = mask * (coupled[0, z, :, cols] - DT * (plus - own))
        updated[1, z, :, cols] = mask * (coupled[1, z, :, cols] - DT * (north - own))
        updated[2, z, :, cols] = mask * (coupled[2, z, :, cols] - DT * (top - own))
        return carry

    lax.fori_loop(0, LEVELS * blocks, project, 0)


def local(velocity, viscosity, heights, row_offset, column_offset):
    flow, viscous, roofs = velocity[0], viscosity[0], heights[0]
    columns = flow.shape[-1]
    group = lax.axis_size("gx")
    x_total = group * ROWS
    tiles = columns // LANES
    half = columns // 2
    t = {name: jnp.asarray(value) for name, value in tables(x_total, columns, group).items()}
    params = lambda size: pltpu.CompilerParams(vmem_limit_bytes=size * MIB)
    effects = lambda number, size: pltpu.CompilerParams(
        has_side_effects=True, collective_id=number, vmem_limit_bytes=size * MIB
    )
    shape = lambda *dims: jax.ShapeDtypeStruct(dims, f32)
    vmem = pltpu.VMEM
    dma = pltpu.SemaphoreType.DMA

    west, east, flow, viscous = pl.pallas_call(
        halo_kernel,
        out_shape=[shape(4, LEVELS, columns)] * 2 + [shape(*flow.shape), shape(*viscous.shape)],
        in_specs=[ANY_SPEC] * 2,
        out_specs=[VMEM_SPEC] * 4,
        scratch_shapes=[vmem((2, 4, LEVELS, columns), f32), dma((8,))],
        compiler_params=effects(0, 10),
        name="halo",
    )(flow, viscous)
    prov, chunks = pl.pallas_call(
        stencil_kernel,
        out_shape=[shape(3, LEVELS, ROWS, columns), shape(24, ROWS, half)],
        in_specs=[SMEM_SPEC] + [VMEM_SPEC] * 6,
        out_specs=[VMEM_SPEC] * 2,
        scratch_shapes=[vmem((24 * 8, columns), f32), vmem((tiles, ROWS, LANES), f32)],
        compiler_params=params(14),
        name="stencil",
    )(column_offset, flow, viscous, roofs, west, east, t["pair"])
    beside = pl.pallas_call(
        align_kernel,
        out_shape=shape(24, 8, half),
        in_specs=[VMEM_SPEC],
        out_specs=VMEM_SPEC,
        scratch_shapes=[dma((2,))],
        compiler_params=effects(1, 6),
        name="align",
    )(chunks)
    even, odd = pl.pallas_call(
        shift_kernel,
        out_shape=[shape(216, half)] * 2,
        in_specs=[SMEM_SPEC] + [VMEM_SPEC] * 2,
        out_specs=[VMEM_SPEC] * 2,
        compiler_params=params(8),
        name="shift",
    )(row_offset, chunks, beside)
    even, odd = lax.switch(
        row_offset[0] // 8,
        [functools.partial(cross, number, effects(3 + number, 6)) for number in range(group + 1)],
        even,
        odd,
    )
    coupled, spectrum, ends, y_t = pl.pallas_call(
        forward_kernel,
        out_shape=[
            shape(3, LEVELS, ROWS, columns),
            shape(EXTRA, columns),
            shape(2 * tiles, 8, LANES),
            jax.ShapeDtypeStruct((4, half, half), bf16),
        ],
        in_specs=[SMEM_SPEC] * 2 + [VMEM_SPEC] * 7 + [ANY_SPEC],
        out_specs=[VMEM_SPEC] * 4,
        scratch_shapes=[
            vmem((24, tiles, ROWS, LANES), f32),
            vmem((216, columns), f32),
            vmem((ROWS, columns), f32),
            vmem((EXTRA, columns), f32),
            vmem((EXTRA, columns), f32),
            dma((4,)),
        ],
        compiler_params=params(32),
        name="forward",
    )(row_offset, column_offset, prov, even, odd, roofs, t["wide"], t["turn"], t["modes"], t["y"])
    share = 2 * tiles // TEAM
    incoming = pl.pallas_call(
        chain_kernel,
        out_shape=shape(TEAM, share, 8, LANES),
        in_specs=[VMEM_SPEC] * 2,
        out_specs=VMEM_SPEC,
        scratch_shapes=[
            vmem((TEAM, share, 8, LANES), f32),
            vmem((group // TEAM, share, 8, LANES), f32),
            vmem((TEAM, share, 8, LANES), f32),
            dma((6,)),
        ],
        compiler_params=effects(2, 4),
        name="chain",
    )(ends.reshape(TEAM, share, 8, LANES), t["jump"])
    incoming = incoming.reshape(2 * tiles, 8, LANES)
    updated, pressure = pl.pallas_call(
        backward_kernel,
        out_shape=[shape(3, LEVELS, ROWS, columns), shape(LEVELS, ROWS, columns)],
        in_specs=[VMEM_SPEC] * 7,
        out_specs=[VMEM_SPEC] * 2,
        scratch_shapes=[
            vmem((EXTRA, columns), f32),
            vmem((EXTRA, columns), f32),
            vmem((LEVELS, columns), f32),
        ],
        compiler_params=params(24),
        name="backward",
    )(coupled, spectrum, incoming, roofs, t["back"], t["modes"], y_t)
    return updated[None], pressure[None]


def solution(mesh):
    return jax.shard_map(
        local,
        mesh=mesh,
        in_specs=(
            P("nest", None, None, "gx", None),
            P("nest", None, "gx", None),
            P("nest", "gx", None),
            P(),
            P(),
        ),
        out_specs=(P("nest", None, None, "gx", None), P("nest", None, "gx", None)),
        check_vma=False,
    )
```

```python
import functools
import math

import jax
import jax.numpy as jnp
import ml_dtypes
import numpy as np
from jax import lax
from jax.experimental import pallas as pl
from jax.experimental.pallas import tpu as pltpu
from jax.sharding import PartitionSpec as P

LEVELS = 8
ROWS = 16
LANES = 128
EXTRA = 144
TEAM = 8
DT = 0.2
BLEND = 0.5
f32 = jnp.float32
bf16 = jnp.bfloat16
VMEM_SPEC = pl.BlockSpec(memory_space=pltpu.VMEM)
SMEM_SPEC = pl.BlockSpec(memory_space=pltpu.SMEM)
ANY_SPEC = pl.BlockSpec(memory_space=pl.ANY)
MIB = 1024 * 1024


def split_np(table):
    high = table.astype(ml_dtypes.bfloat16)
    low = (table - high.astype(np.float64)).astype(ml_dtypes.bfloat16)
    return high, low


def split(value):
    high = value.astype(bf16)
    low = (value - high.astype(f32)).astype(bf16)
    return high, low


def cas(angle):
    return np.cos(angle) + np.sin(angle)


@functools.lru_cache(maxsize=None)
def tables(x_total, columns, group):
    half = columns // 2
    m = np.arange(half)
    even = cas(2 * np.pi * ((m[:, None] * m[None, :]) % half) / half)
    odd_index = ((2 * m[:, None] + 1) * (2 * m[None, :] + 1)) % (2 * columns)
    odd = cas(2 * np.pi * odd_index / (2 * columns))
    even_high, even_low = split_np(even)
    odd_high, odd_low = split_np(odd)
    y_tables = np.stack([even_high, even_low, odd_high, odd_low])
    j = np.arange(LEVELS)
    z_vectors = math.sqrt(4 / 17) * np.cos((2 * j[:, None] + 1) * (2 * j[None, :] + 1) * np.pi / 34)
    z_values = 2 - 2 * np.cos((2 * j + 1) * np.pi / 17)
    turn = np.zeros((EXTRA, EXTRA))
    for x in range(ROWS + 1):
        for level in range(LEVELS):
            place = level * ROWS + x if x < ROWS else ROWS * LEVELS + level
            turn[x * LEVELS : x * LEVELS + LEVELS, place] = z_vectors[:, level]
    turn_high, turn_low = split_np(turn)
    back_high, back_low = split_np(turn.T)
    turn_stack = np.concatenate([turn_high, turn_low])
    back_stack = np.concatenate([back_high, back_low])
    wave = np.concatenate([2 * m, 2 * m + 1])
    mu = 4 * np.sin(np.pi * wave / columns)[None, :] ** 2 + z_values[:, None]
    root = 1 + mu / 2 - np.sqrt(mu + mu * mu / 4)
    scale = -1 / (1 / root - root) / columns
    modes = np.stack([root, scale]).astype(np.float32)
    reach = root**ROWS
    tiles = columns // LANES
    jump = np.stack([reach, reach**TEAM, 1 / (1 - reach**group)])
    jump = jump.reshape(3, LEVELS, tiles, LANES).transpose(0, 2, 1, 3).astype(np.float32)
    wide = np.zeros((2, 256, 256))
    for y in range(256):
        if y % 2 == 0:
            wide[:, y // 2, y] = 1
        else:
            wide[:, y // 2, y] = 0.5
            wide[0, y // 2 + 1, y] = 0.5
            wide[1, min(y // 2 + 1, 127), y] += 0.5
    pair = np.zeros((256, LANES))
    pair[np.arange(256), np.arange(256) // 2] = 0.5
    return dict(
        y=y_tables,
        turn=turn_stack,
        back=back_stack,
        modes=modes,
        jump=jump,
        wide=wide.astype(ml_dtypes.bfloat16),
        pair=pair.astype(ml_dtypes.bfloat16),
    )


def mxu(left, right):
    return jnp.dot(left, right, preferred_element_type=f32)


def greet(nest, k):
    pl.semaphore_signal(
        pltpu.get_barrier_semaphore(), inc=1, device_id={"nest": nest, "gx": k},
        device_id_type=pl.DeviceIdType.MESH,
    )


def halo_kernel(vel_any, visc_any, west, east, vel, visc, edge, sems):
    me = lax.axis_index("gx")
    nest = lax.axis_index("nest")
    group = lax.axis_size("gx")
    right = lax.rem(me + 1, group)
    left = lax.rem(me + group - 1, group)
    greet(nest, left)
    greet(nest, right)
    loads = [pltpu.make_async_copy(vel_any.at[c], vel.at[c], sems.at[4 + c]) for c in range(3)]
    loads.append(pltpu.make_async_copy(visc_any, visc, sems.at[7]))
    for load in loads:
        load.start()
    for load in loads:
        load.wait()
    for c in range(3):
        edge[0, c] = vel[c, :, 0, :]
        edge[1, c] = vel[c, :, ROWS - 1, :]
    edge[0, 3] = visc[:, 0, :]
    edge[1, 3] = visc[:, ROWS - 1, :]
    pl.semaphore_wait(pltpu.get_barrier_semaphore(), 2)
    to_right = pltpu.make_async_remote_copy(
        edge.at[1], west, sems.at[0], sems.at[1], device_id={"gx": right},
        device_id_type=pl.DeviceIdType.MESH,
    )
    to_left = pltpu.make_async_remote_copy(
        edge.at[0], east, sems.at[2], sems.at[3], device_id={"gx": left},
        device_id_type=pl.DeviceIdType.MESH,
    )
    to_right.start()
    to_left.start()
    to_right.wait()
    to_left.wait()


def stencil_kernel(oy_ref, vel, visc, heights, west, east, pair, prov, out, mean, tile):
    columns = vel.shape[-1]
    tiles = columns // LANES
    blocks = columns // 256
    is_child = lax.axis_index("nest") == 1
    row = lax.broadcasted_iota(jnp.int32, (ROWS, 256), 0)
    lane = lax.broadcasted_iota(jnp.int32, (ROWS, LANES), 1)

    def cell(i, carry):
        z = i // blocks
        start = pl.multiple_of(lax.rem(i, blocks) * 256, 256)
        here = pl.ds(start, 256)
        before = pl.ds(pl.multiple_of(lax.rem(start + columns - LANES, columns), LANES), LANES)
        after = pl.ds(pl.multiple_of(lax.rem(start + 256, columns), LANES), LANES)
        up = jnp.minimum(z + 1, LEVELS - 1)
        down = jnp.maximum(z - 1, 0)
        up_open = jnp.where(z < LEVELS - 1, 1.0, 0.0).astype(f32)
        down_open = jnp.where(z > 0, 1.0, 0.0).astype(f32)

        def around(ref, lead, c):
            mid = ref[lead + (z, slice(None), here)]
            wide = jnp.concatenate(
                [ref[lead + (z, slice(None), before)], mid, ref[lead + (z, slice(None), after)]],
                axis=1,
            )
            north = pltpu.roll(wide, 511, 1)[:, LANES : LANES + 256]
            south = pltpu.roll(wide, 1, 1)[:, LANES : LANES + 256]
            plus = jnp.where(row == ROWS - 1, east[c, pl.ds(z, 1), here], pltpu.roll(mid, ROWS - 1, 0))
            minus = jnp.where(row == 0, west[c, pl.ds(z, 1), here], pltpu.roll(mid, 1, 0))
            top = ref[lead + (up, slice(None), here)]
            bottom = ref[lead + (down, slice(None), here)]
            return mid, plus, minus, north, south, top, bottom

        k, ke, kw, kn, ks, kt, kb = around(visc, (), 3)
        flow = [around(vel, (c,), c) for c in range(3)]
        half = 0.5 * DT
        kh = half * k
        b0, b1, b2 = (half * flow[c][0] for c in range(3))
        ae = (kh + half * ke) - b0
        aw = (kh + half * kw) + b0
        an = (kh + half * kn) - b1
        as_ = (kh + half * ks) + b1
        at = (kh + half * kt) - b2
        ab = (kh + half * kb) + b2
        mask = jnp.where(z >= heights[:, here], 1.0, 0.0).astype(f32)
        own = 1.0 - (((ae + aw) + (an + as_)) + (at + ab))
        at = at * up_open
        ab = ab * down_open
        for c in range(3):
            mid, plus, minus, north, south, top, bottom = flow[c]
            value = own * mid + ae * plus + aw * minus + an * north + as_ * south + at * top + ab * bottom
            prov[c, z, :, here] = value * mask
        return carry

    lax.fori_loop(0, LEVELS * blocks, cell, 0, unroll=2)

    @pl.when(jnp.logical_not(is_child))
    def _():
        oy = oy_ref[0]
        first = oy // LANES
        shift = lax.rem(oy, LANES)
        turn = lax.rem(LANES - shift, LANES)

        def unit(cz, carry):
            c = cz // LEVELS
            z = lax.rem(cz, LEVELS)
            moved = []
            for b in range(blocks + 1):
                cols = pl.ds(pl.multiple_of(lax.rem(first + b, tiles) * LANES, LANES), LANES)
                moved.append(pltpu.roll(prov[c, z, :, cols], turn, 1))
            for b in range(blocks):
                out[cz, :, pl.ds(b * LANES, LANES)] = jnp.where(lane < LANES - shift, moved[b], moved[b + 1])
            return carry

        lax.fori_loop(0, 24, unit, 0, unroll=2)

    @pl.when(is_child)
    def _():
        def rows(cz, carry):
            c = cz // LEVELS
            z = lax.rem(cz, LEVELS)
            for t in range(tiles):
                cols = pl.ds(t * LANES, LANES)
                tile[t] = prov[c, z, :, cols]
                evens = tile[t, pl.ds(0, 8, stride=2), :]
                odds = tile[t, pl.ds(1, 8, stride=2), :]
                mean[pl.ds(pl.multiple_of(cz * 8, 8), 8), cols] = 0.5 * (evens + odds)
            return carry

        lax.fori_loop(0, 24, rows, 0)
        for b in range(blocks):
            high, low = split(mean[:, pl.ds(b * 256, 256)])
            value = mxu(high, pair[...]) + mxu(low, pair[...])
            out[:, pl.ds(0, 8), pl.ds(b * LANES, LANES)] = value.reshape(24, 8, LANES)


def remote(src, dst, send, recv, nest, k):
    return pltpu.make_async_remote_copy(
        src, dst, send, recv, device_id={"nest": nest, "gx": k},
        device_id_type=pl.DeviceIdType.MESH,
    )


def await_bytes(ref, sem):
    pltpu.make_async_copy(ref, ref, sem).wait()


def align_kernel(src, beside, sems):
    me = lax.axis_index("gx")
    nest = lax.axis_index("nest")
    group = lax.axis_size("gx")
    step = jnp.where(nest == 0, group - 1, 1)
    target = lax.rem(me + step, group)
    greet(nest, lax.rem(me + group - step, group))
    pl.semaphore_wait(pltpu.get_barrier_semaphore(), 1)
    copy = remote(src.at[:, pl.ds(0, 8)], beside, sems.at[0], sems.at[1], nest, target)
    copy.start()
    copy.wait()


def shift_kernel(ox_ref, own, beside, even, odd):
    group = lax.axis_size("gx")
    half = own.shape[-1]
    me = lax.axis_index("gx")
    ox = ox_ref[0]
    rest = lax.rem(ox, 8)
    parity = lax.rem(ox // 8 + me, 2)

    @pl.when(lax.axis_index("nest") == 0)
    def _():
        def fill(i, carry):
            for b in range(half // LANES):
                cols = pl.ds(b * LANES, LANES)
                ninths = ([], [])
                for j in range(8):
                    cz = i * 8 + j
                    rows = jnp.concatenate([own[cz, :, cols], beside[cz, :, cols]], axis=0)
                    rows = pltpu.roll(rows, lax.rem(24 - rest, 24), 0)
                    place = pl.ds(pl.multiple_of(cz * 8, 8), 8)
                    even[place, cols] = rows[:8]
                    odd[place, cols] = rows[8:16]
                    ninths[0].append(rows[8:9])
                    ninths[1].append(rows[16:17])
                place = pl.ds(pl.multiple_of(192 + i * 8, 8), 8)
                even[place, cols] = jnp.concatenate(ninths[0], axis=0)
                odd[place, cols] = jnp.concatenate(ninths[1], axis=0)
            return carry

        lax.fori_loop(0, 3, fill, 0)

    @pl.when(lax.axis_index("nest") == 1)
    def _():
        mine = jnp.full((8, LANES), parity, jnp.int32) == 0

        def fill(cz, carry):
            place = pl.ds(pl.multiple_of(cz * 8, 8), 8)
            for b in range(half // LANES):
                cols = pl.ds(b * LANES, LANES)
                value = own[cz, pl.ds(0, 8), cols]
                rows = jnp.concatenate([value, beside[cz, :, cols]], axis=0)
                rows = pltpu.roll(rows, rest, 0)
                even[place, cols] = jnp.where(mine, rows[:8], rows[8:])
                odd[place, cols] = jnp.where(mine, rows[8:], rows[:8])
            return carry

        lax.fori_loop(0, 24, fill, 0)


def cross_kernel(shift, even, odd, even_in, odd_in, sems):
    group = lax.axis_size("gx")
    me = lax.axis_index("gx")
    nest = lax.axis_index("nest")
    barrier = pltpu.get_barrier_semaphore()
    sources = (even, odd)
    targets = (even_in, odd_in)
    means = pl.ds(0, 192)
    last = group - 1
    spill = shift < group

    def greet_nest(other, k):
        pl.semaphore_signal(
            barrier, inc=1, device_id={"nest": other, "gx": k}, device_id_type=pl.DeviceIdType.MESH
        )

    @pl.when(nest == 0)
    def _():
        for e in range(2):
            g = 2 * me + e - shift

            @pl.when((g >= 0) & (g < group))
            def _():
                greet_nest(1, g)

            if spill:
                @pl.when(g == group)
                def _():
                    greet_nest(1, last)

        count = jnp.int32(0)
        for e in range(2):
            g = 2 * me + e - shift
            count = count + jnp.where((g >= 0) & (g < group), 1, 0)

        @pl.when(count > 0)
        def _():
            pl.semaphore_wait(barrier, count)

        for e in range(2):
            g = 2 * me + e - shift

            @pl.when((g >= 0) & (g < group))
            def _():
                remote(sources[e], targets[e], sems.at[0, e], sems.at[1, e], 1, g).start()

        for e in range(2):
            g = 2 * me + e - shift
            take = (g >= 0) & (g < group)

            @pl.when(take)
            def _():
                await_bytes(sources[e], sems.at[0, e])

            @pl.when(take | (g == group) if spill else take)
            def _():
                await_bytes(targets[e].at[means], sems.at[1, e])

    @pl.when(nest == 1)
    def _():
        block = shift + me
        q = block // 2
        e_mine = lax.rem(block, 2)
        greet_nest(0, q)
        pl.semaphore_wait(barrier, jnp.where(me == last, 2, 1) if spill else 1)
        if spill:
            @pl.when(me == last)
            def _():
                e = shift % 2
                k = (shift + group) // 2
                remote(sources[e].at[means], targets[e].at[means], sems.at[0, e], sems.at[1, e], 0, k).start()

        for e in range(2):
            @pl.when(e_mine == e)
            def _():
                remote(sources[e].at[means], targets[e].at[means], sems.at[0, e], sems.at[1, e], 0, q).start()

        for e in range(2):
            @pl.when(e_mine == e)
            def _():
                await_bytes(sources[e].at[means], sems.at[0, e])
                await_bytes(targets[e], sems.at[1, e])

        if spill:
            @pl.when(me == last)
            def _():
                await_bytes(sources[shift % 2].at[means], sems.at[0, shift % 2])


def cross(shift, params, even, odd):
    return pl.pallas_call(
        functools.partial(cross_kernel, shift),
        out_shape=[jax.ShapeDtypeStruct(even.shape, f32)] * 2,
        in_specs=[VMEM_SPEC] * 2,
        out_specs=[VMEM_SPEC] * 2,
        scratch_shapes=[pltpu.SemaphoreType.DMA((2, 2))],
        compiler_params=params,
        name="cross",
    )(even, odd)


def forward_kernel(
    ox_ref, oy_ref, prov, even, odd, heights, wide_t, turn_t, modes, y_any,
    coupled, spectrum, ends, y_t, mapped, wide, rate, source, turned, sems,
):
    columns = prov.shape[-1]
    loads = [pltpu.make_async_copy(y_any.at[i], y_t.at[i], sems.at[i]) for i in range(4)]
    for load in loads:
        load.start()
    group = lax.axis_size("gx")
    x_total = group * ROWS
    half = columns // 2
    tiles = columns // LANES
    blocks = columns // 256
    me = lax.axis_index("gx")
    is_child = lax.axis_index("nest") == 1
    ox = ox_ref[0]
    oy = oy_ref[0]
    lane = lax.broadcasted_iota(jnp.int32, (ROWS, LANES), 1)
    row = lax.broadcasted_iota(jnp.int32, (ROWS, LANES), 0)

    @pl.when(is_child)
    def _():
        first_is_even = jnp.full((216, LANES), lax.rem(ox // 8 + me, 2), jnp.int32) == 0

        def block(b):
            cols = pl.ds(b * LANES, LANES)
            return jnp.where(first_is_even, even[:, cols], odd[:, cols])

        left = block(0)
        for b in range(blocks):
            right = block(min(b + 1, blocks - 1))
            high, low = split(jnp.concatenate([left, right], axis=1))
            table = wide_t[0 if b < blocks - 1 else 1]
            wide[:, pl.ds(b * 256, 256)] = mxu(high, table) + mxu(low, table)
            left = right
        tail = lax.broadcasted_iota(jnp.int32, (8, LANES), 0) == 7
        last = jnp.full((8, LANES), me, jnp.int32) == group - 1

        def unit(i, carry):
            for t in range(tiles):
                cols = pl.ds(t * LANES, LANES)
                ninths = wide[pl.ds(pl.multiple_of(192 + i * 8, 8), 8), cols]
                for j in range(8):
                    cz = i * 8 + j
                    own = wide[pl.ds(pl.multiple_of(cz * 8, 8), 8), cols]
                    ninth = jnp.where(last, own, ninths[j : j + 1])
                    after = jnp.where(tail, ninth, pltpu.roll(own, 7, 0))
                    mapped[cz, t, pl.ds(0, 8, stride=2), :] = own
                    mapped[cz, t, pl.ds(1, 8, stride=2), :] = 0.5 * (own + after)
            return carry

        lax.fori_loop(0, 3, unit, 0)

        def rates(t, carry):
            cols = pl.ds(pl.multiple_of(t * LANES, LANES), LANES)
            x = me * ROWS + row
            y = t * LANES + lane
            near_y = jnp.minimum(y, columns - 1 - y)
            near_x = jnp.minimum(x, x_total - 1 - x)
            near = jnp.minimum(near_x, near_y).astype(f32)
            rate[:, cols] = 0.2 + 0.8 * jnp.exp(-near * (16.0 / columns))
            return carry

        lax.fori_loop(0, tiles, rates, 0)

    @pl.when(jnp.logical_not(is_child))
    def _():
        first = oy // LANES
        shift = lax.rem(oy, LANES)

        def unit(cz, carry):
            rows = pl.ds(pl.multiple_of(cz * 8, 8), 8)
            moved = []
            for b in range(blocks):
                cols = pl.ds(b * LANES, LANES)
                both = jnp.concatenate([even[rows, cols], odd[rows, cols]], axis=0)
                moved.append(pltpu.roll(both, shift, 1))
            for b in range(blocks + 1):
                own = moved[min(b, blocks - 1)]
                before = moved[max(b - 1, 0)]
                mapped[cz, lax.rem(first + b, tiles)] = jnp.where(lane >= shift, own, before)
            return carry

        lax.fori_loop(0, 24, unit, 0, unroll=2)

        def rates(t, carry):
            cols = pl.ds(pl.multiple_of(t * LANES, LANES), LANES)
            x = me * ROWS + row
            y = t * LANES + lane
            j = y - oy
            j = jnp.where(j < 0, j + columns, j)
            inside = (x >= ox) & (x < ox + x_total // 2) & (j < half)
            rate[:, cols] = jnp.where(inside, BLEND, 0.0)
            return carry

        lax.fori_loop(0, tiles, rates, 0)

    source[pl.ds(ROWS * LEVELS, ROWS), :] = jnp.zeros((ROWS, columns), f32)

    def blend(i, carry):
        z = i // blocks
        b = lax.rem(i, blocks)
        cols = pl.ds(pl.multiple_of(b * 256, 256), 256)
        weight = rate[:, cols]
        mask = jnp.where(z >= heights[:, cols], 1.0, 0.0).astype(f32)
        for c in range(3):
            own = prov[c, z, :, cols]
            other = jnp.concatenate([mapped[c * LEVELS + z, 2 * b], mapped[c * LEVELS + z, 2 * b + 1]], axis=1)
            change = jnp.where(weight > 0.0, other - own, 0.0)
            coupled[c, z, :, cols] = (own + weight * change) * mask
        return carry

    lax.fori_loop(0, LEVELS * blocks, blend, 0, unroll=4)
    row2 = lax.broadcasted_iota(jnp.int32, (ROWS, 256), 0)

    def diverge(i, carry):
        z = i // blocks
        start = pl.multiple_of(lax.rem(i, blocks) * 256, 256)
        cols = pl.ds(start, 256)
        before = pl.ds(pl.multiple_of(lax.rem(start + columns - LANES, columns), LANES), LANES)
        flow_x = coupled[0, z, :, cols]
        flow_y = coupled[1, z, :, cols]
        flow_z = coupled[2, z, :, cols]
        beyond = jnp.concatenate([coupled[1, z, :, before], flow_y], axis=1)
        south = pltpu.roll(beyond, 1, 1)[:, LANES:]
        west = jnp.where(row2 == 0, 0.0, pltpu.roll(flow_x, 1, 0))
        under = coupled[2, jnp.maximum(z - 1, 0), :, cols] * jnp.where(z > 0, 1.0, 0.0).astype(f32)
        value = ((flow_x - west) + (flow_y - south)) + (flow_z - under)
        source[pl.ds(pl.multiple_of(z * ROWS, ROWS), ROWS), cols] = value * (1.0 / DT)
        source[pl.ds(ROWS * LEVELS + z, 1), cols] = flow_x[ROWS - 1 :] * (-1.0 / DT)
        return carry

    lax.fori_loop(0, LEVELS * blocks, diverge, 0, unroll=4)

    def turning(b, carry):
        cols = pl.ds(pl.multiple_of(b * 256, 256), 256)
        high, low = split(source[:, cols])
        both = mxu(turn_t[...], high)
        turned[:, cols] = (both[:EXTRA] + both[EXTRA:]) + mxu(turn_t[pl.ds(0, EXTRA), :], low)
        return carry

    lax.fori_loop(0, blocks, turning, 0)
    for load in loads:
        load.wait()
    width = min(half, 256)
    for part in range(2):
        one = turned[:, pl.ds(0, half)]
        two = turned[:, pl.ds(half, half)]
        high, low = split(one + two if part == 0 else one - two)
        stacked = jnp.concatenate([high, low], axis=0)

        def transform(b, carry):
            cols = pl.ds(pl.multiple_of(b * width, width), width)
            both = mxu(stacked, y_t[2 * part, :, cols])
            value = (both[:EXTRA] + both[EXTRA:]) + mxu(high, y_t[2 * part + 1, :, cols])
            spectrum[:, pl.ds(pl.multiple_of(part * half + b * width, width), width)] = value
            return carry

        lax.fori_loop(0, half // width, transform, 0)

    def scans(t, carry):
        cols = pl.ds(pl.multiple_of(t * LANES, LANES), LANES)
        root = modes[0, :, cols]
        lead = spectrum[pl.ds(0, 8), cols]
        for x in range(1, ROWS + 1):
            lead = spectrum[pl.ds(8 * x, 8), cols] + root * lead
        trail = spectrum[pl.ds(8 * ROWS, 8), cols]
        for x in range(ROWS - 1, -1, -1):
            trail = spectrum[pl.ds(8 * x, 8), cols] + root * trail
        ends[t] = lead
        ends[tiles + t] = trail
        return carry

    lax.fori_loop(0, tiles, scans, 0)


def chain_kernel(ends, jump, dst, held, sums, result, sems):
    me = lax.axis_index("gx")
    nest = lax.axis_index("nest")
    size, share = ends.shape[:2]
    teams = sums.shape[0]
    tiles = jump.shape[1]
    team = me // size
    seat = lax.rem(me, size)
    near = [team * size + lax.rem(seat + i, size) for i in range(1, size)]
    far = [lax.rem(team + i, teams) * size + seat for i in range(1, teams)]
    for k in near + far:
        greet(nest, k)
    pl.semaphore_wait(pltpu.get_barrier_semaphore(), len(near) + len(far))
    for i in range(1, size):
        other = lax.rem(seat + i, size)
        remote(ends.at[other], held.at[seat], sems.at[0], sems.at[1], nest, team * size + other).start()
    held[seat] = ends[seat]
    first = seat * share
    back = first >= tiles
    own = pl.ds(jnp.where(back, first - tiles, first), share)
    ratio = jump[0, own]
    await_bytes(held.at[pl.ds(0, size - 1)], sems.at[1])

    def place(i):
        return jnp.where(back, size - 1 - i, i)

    total = held[place(0)]
    for i in range(1, size):
        total = total * ratio + held[place(i)]
    sums[team] = total
    for i in range(1, teams):
        k = lax.rem(team + i, teams) * size + seat
        remote(sums.at[team], sums.at[team], sems.at[2], sems.at[3], nest, k).start()
    await_bytes(sums.at[pl.ds(0, teams - 1)], sems.at[3])
    value = total
    for i in range(1, teams):
        at = jnp.where(back, lax.rem(team + teams - i, teams), lax.rem(team + i, teams))
        value = value * jump[1, own] + sums[at]
    value = value * jump[2, own]
    for i in range(size):
        g = place(i)
        result[g] = value
        if i < size - 1:
            value = held[g] + ratio * value
    for i in range(1, size):
        other = lax.rem(seat + i, size)
        remote(result.at[other], dst.at[seat], sems.at[4], sems.at[5], nest, team * size + other).start()
    dst[seat] = result[seat]
    await_bytes(ends.at[pl.ds(0, size - 1)], sems.at[0])
    await_bytes(sums.at[pl.ds(0, teams - 1)], sems.at[2])
    await_bytes(result.at[pl.ds(0, size - 1)], sems.at[4])
    await_bytes(dst.at[pl.ds(0, size - 1)], sems.at[5])


def backward_kernel(
    coupled, spectrum, incoming, heights, back_t, modes, y_t,
    updated_out, pressure_out, waves, folded, east, updated, pressure, sems,
):
    columns = coupled.shape[-1]
    half = columns // 2
    tiles = columns // LANES
    blocks = columns // 256
    waves[pl.ds(8 * (ROWS + 1), 8), :] = jnp.zeros((8, columns), f32)

    def scans(t, carry):
        cols = pl.ds(pl.multiple_of(t * LANES, LANES), LANES)
        root = modes[0, :, cols]
        scale = modes[1, :, cols]
        trail = spectrum[pl.ds(8 * ROWS, 8), cols] + incoming[tiles + t]
        trails = [trail]
        for x in range(ROWS - 1, 0, -1):
            trail = spectrum[pl.ds(8 * x, 8), cols] + root * trail
            trails.append(trail)
        lead = incoming[t] + spectrum[pl.ds(0, 8), cols]
        for x in range(ROWS):
            if x:
                lead = spectrum[pl.ds(8 * x, 8), cols] + root * lead
            waves[pl.ds(8 * x, 8), cols] = (lead + root * trails[ROWS - 1 - x]) * scale
        waves[pl.ds(8 * ROWS, 8), cols] = (root * lead + trails[0]) * scale
        return carry

    lax.fori_loop(0, tiles, scans, 0)
    width = min(half, 256)
    parts = []
    for part in range(2):
        high, low = split(waves[:, pl.ds(part * half, half)])
        parts.append((jnp.concatenate([high, low], axis=0), high))

    def transform(b, carry):
        cols = pl.ds(pl.multiple_of(b * width, width), width)
        values = []
        for part in range(2):
            stacked, high = parts[part]
            both = mxu(stacked, y_t[2 * part, :, cols])
            values.append((both[:EXTRA] + both[EXTRA:]) + mxu(high, y_t[2 * part + 1, :, cols]))
        folded[:, cols] = values[0] + values[1]
        folded[:, pl.ds(pl.multiple_of(half + b * width, width), width)] = values[0] - values[1]
        return carry

    lax.fori_loop(0, half // width, transform, 0)

    def turning(b, carry):
        cols = pl.ds(pl.multiple_of(b * 256, 256), 256)
        high, low = split(folded[:, cols])
        both = mxu(back_t[...], high)
        value = (both[:EXTRA] + both[EXTRA:]) + mxu(back_t[pl.ds(0, EXTRA), :], low)
        pressure[:, :, cols] = value[: ROWS * LEVELS].reshape(LEVELS, ROWS, 256)
        east[:, cols] = value[ROWS * LEVELS : ROWS * LEVELS + LEVELS]
        return carry

    lax.fori_loop(0, blocks, turning, 0)
    stores = [pltpu.make_async_copy(pressure, pressure_out, sems.at[LEVELS])]
    stores[0].start()
    row = lax.broadcasted_iota(jnp.int32, (ROWS, 256), 0)

    def project(z, b, carry):
        start = pl.multiple_of(b * 256, 256)
        cols = pl.ds(start, 256)
        after = pl.ds(pl.multiple_of(lax.rem(start + 256, columns), LANES), LANES)
        own = pressure[z, :, cols]
        beyond = jnp.concatenate([own, pressure[z, :, after]], axis=1)
        north = pltpu.roll(beyond, 383, 1)[:, :256]
        plus = jnp.where(row == ROWS - 1, east[pl.ds(z, 1), cols], pltpu.roll(own, ROWS - 1, 0))
        top = pressure[z + 1, :, cols] if z < LEVELS - 1 else jnp.zeros_like(own)
        mask = jnp.where(z >= heights[:, cols], 1.0, 0.0).astype(f32)
        updated[0, z, :, cols] = mask * (coupled[0, z, :, cols] - DT * (plus - own))
        updated[1, z, :, cols] = mask * (coupled[1, z, :, cols] - DT * (north - own))
        updated[2, z, :, cols] = mask * (coupled[2, z, :, cols] - DT * (top - own))
        return carry

    for z in range(LEVELS):
        lax.fori_loop(0, blocks, functools.partial(project, z), 0, unroll=2)
        stores.append(pltpu.make_async_copy(updated.at[:, z], updated_out.at[:, z], sems.at[z]))
        stores[-1].start()
    for store in stores:
        store.wait()


def local(velocity, viscosity, heights, row_offset, column_offset):
    flow, viscous, roofs = velocity[0], viscosity[0], heights[0]
    columns = flow.shape[-1]
    group = lax.axis_size("gx")
    x_total = group * ROWS
    tiles = columns // LANES
    half = columns // 2
    t = {name: jnp.asarray(value) for name, value in tables(x_total, columns, group).items()}
    params = lambda size: pltpu.CompilerParams(vmem_limit_bytes=size * MIB)
    effects = lambda number, size: pltpu.CompilerParams(
        has_side_effects=True, collective_id=number, vmem_limit_bytes=size * MIB
    )
    shape = lambda *dims: jax.ShapeDtypeStruct(dims, f32)
    vmem = pltpu.VMEM
    dma = pltpu.SemaphoreType.DMA

    west, east, flow, viscous = pl.pallas_call(
        halo_kernel,
        out_shape=[shape(4, LEVELS, columns)] * 2 + [shape(*flow.shape), shape(*viscous.shape)],
        in_specs=[ANY_SPEC] * 2,
        out_specs=[VMEM_SPEC] * 4,
        scratch_shapes=[vmem((2, 4, LEVELS, columns), f32), dma((8,))],
        compiler_params=effects(0, 10),
        name="halo",
    )(flow, viscous)
    prov, chunks = pl.pallas_call(
        stencil_kernel,
        out_shape=[shape(3, LEVELS, ROWS, columns), shape(24, ROWS, half)],
        in_specs=[SMEM_SPEC] + [VMEM_SPEC] * 6,
        out_specs=[VMEM_SPEC] * 2,
        scratch_shapes=[vmem((24 * 8, columns), f32), vmem((tiles, ROWS, LANES), f32)],
        compiler_params=params(14),
        name="stencil",
    )(column_offset, flow, viscous, roofs, west, east, t["pair"])
    beside = pl.pallas_call(
        align_kernel,
        out_shape=shape(24, 8, half),
        in_specs=[VMEM_SPEC],
        out_specs=VMEM_SPEC,
        scratch_shapes=[dma((2,))],
        compiler_params=effects(1, 6),
        name="align",
    )(chunks)
    even, odd = pl.pallas_call(
        shift_kernel,
        out_shape=[shape(216, half)] * 2,
        in_specs=[SMEM_SPEC] + [VMEM_SPEC] * 2,
        out_specs=[VMEM_SPEC] * 2,
        compiler_params=params(8),
        name="shift",
    )(row_offset, chunks, beside)
    even, odd = lax.switch(
        row_offset[0] // 8,
        [functools.partial(cross, number, effects(3 + number, 6)) for number in range(group + 1)],
        even,
        odd,
    )
    coupled, spectrum, ends, y_t = pl.pallas_call(
        forward_kernel,
        out_shape=[
            shape(3, LEVELS, ROWS, columns),
            shape(EXTRA, columns),
            shape(2 * tiles, 8, LANES),
            jax.ShapeDtypeStruct((4, half, half), bf16),
        ],
        in_specs=[SMEM_SPEC] * 2 + [VMEM_SPEC] * 7 + [ANY_SPEC],
        out_specs=[VMEM_SPEC] * 4,
        scratch_shapes=[
            vmem((24, tiles, ROWS, LANES), f32),
            vmem((216, columns), f32),
            vmem((ROWS, columns), f32),
            vmem((EXTRA, columns), f32),
            vmem((EXTRA, columns), f32),
            dma((4,)),
        ],
        compiler_params=params(32),
        name="forward",
    )(row_offset, column_offset, prov, even, odd, roofs, t["wide"], t["turn"], t["modes"], t["y"])
    share = 2 * tiles // TEAM
    incoming = pl.pallas_call(
        chain_kernel,
        out_shape=shape(TEAM, share, 8, LANES),
        in_specs=[VMEM_SPEC] * 2,
        out_specs=VMEM_SPEC,
        scratch_shapes=[
            vmem((TEAM, share, 8, LANES), f32),
            vmem((group // TEAM, share, 8, LANES), f32),
            vmem((TEAM, share, 8, LANES), f32),
            dma((6,)),
        ],
        compiler_params=effects(2, 4),
        name="chain",
    )(ends.reshape(TEAM, share, 8, LANES), t["jump"])
    incoming = incoming.reshape(2 * tiles, 8, LANES)
    updated, pressure = pl.pallas_call(
        backward_kernel,
        out_shape=[shape(3, LEVELS, ROWS, columns), shape(LEVELS, ROWS, columns)],
        in_specs=[VMEM_SPEC] * 7,
        out_specs=[ANY_SPEC] * 2,
        scratch_shapes=[
            vmem((EXTRA, columns), f32),
            vmem((EXTRA, columns), f32),
            vmem((LEVELS, columns), f32),
            vmem((3, LEVELS, ROWS, columns), f32),
            vmem((LEVELS, ROWS, columns), f32),
            dma((LEVELS + 1,)),
        ],
        compiler_params=params(24),
        name="backward",
    )(coupled, spectrum, incoming, roofs, t["back"], t["modes"], y_t)
    return updated[None], pressure[None]


def solution(mesh):
    return jax.shard_map(
        local,
        mesh=mesh,
        in_specs=(
            P("nest", None, None, "gx", None),
            P("nest", None, "gx", None),
            P("nest", "gx", None),
            P(),
            P(),
        ),
        out_specs=(P("nest", None, None, "gx", None), P("nest", None, "gx", None)),
        check_vma=False,
    )
```
